128 devices in a mesh: section: 2 (over y_hi), wide: 16 (over x, y_lo, core), narrow: 4 (over z).
Axes of the slice: x: 4, y: 4 (y_hi: 2, y_lo: 2; y = y_hi * 2 + y_lo), z: 4, core: 2. Of those that a mesh axis runs over, the one named last changes fastest.
Arguments:
- boundary_grad: bfloat16 [2, 8192, 4096], P('section', 'wide', 'narrow'), may hold values from -6 to 6
- tile_target: int32 [2, 8192], P('section', 'wide'), may hold values from 0 to 15, as said below
- tile_row: int32 [2, 8192], P('section', 'wide'), may hold values from 0 to 511, as said below
- normed_input: bfloat16 [2, 8192, 4096], P('section', 'wide'), may hold values from -6 to 6
- query: bfloat16 [2, 8192, 4096], P('section', 'wide', 'narrow'), may hold values from -16 to 16
- keys: bfloat16 [2, 8192, 4096], P('section', 'wide', 'narrow'), may hold values from -5 to 5
- values: bfloat16 [2, 8192, 4096], P('section', 'wide', 'narrow'), may hold values from -6 to 6
- positions: int32 [2, 8192], P('section', 'wide'), may hold values from 0 to 511, as said below
- out_weight: bfloat16 [2, 4096, 4096], P('section', 'wide', 'narrow'), may hold values from -0.09375 to 0.09375
- value_weight: bfloat16 [2, 4096, 4096], P('section', 'wide', 'narrow'), may hold values from -0.09375 to 0.09375
Outputs:
- grad_input: bfloat16 [2, 8192, 4096], P('section', 'wide')
- grad_query: bfloat16 [2, 8192, 4096], P('section', 'wide', 'narrow')
- grad_key: bfloat16 [2, 8192, 4096], P('section', 'wide', 'narrow')
- grad_out_weight: float32 [2, 4096, 4096], P('section', 'wide', 'narrow')
- grad_value_weight: float32 [2, 4096, 4096], P('section', 'wide', 'narrow')
The draws below stay inside these ranges and needn't reach their ends.
Inputs may be any that keep to these rules, and one draw needn't show every extreme that they name: `tile_target`: each device's 512 rows of a section go to receiving data indices; one device gives at most 48 rows to one index, exactly 48 to some, and every receiving index gets exactly 512 rows from the section. `tile_row`: together with tile_target, names every row of the receiving section exactly once. `positions`: counts the earlier tokens of the same document; documents lie inside aligned blocks of 512 rows, each block's first row has position 0, and each section's first block is one whole document.
All inputs are finite; a program needn't handle non-finite values.
Results may differ from the reference program's by a relative error of at most 0.022.
Values may be sent and summed in bfloat16 or wider, within the bound.
A program may use at most 128 MiB of HBM per device.

```python
import jax
import jax.numpy as jnp
from jax import lax

D = 4096
HEAD_DIM = 128
TOK_DEV = 512
TOKENS = 8192
ATTN_WIDTH = 4096
N_SECTION = 2
N_NARROW = 4


def tile_layout(key):
    groups = TOKENS // TOK_DEV
    mean_load = TOK_DEV // groups
    half_load = mean_load // 2
    pattern = jnp.where(jnp.arange(groups, dtype=jnp.int32) % 2 == 0, half_load, -half_load).astype(jnp.int32)

    def one_section(section_key):
        subkeys = jax.random.split(section_key, 4)
        sigma = jax.random.permutation(subkeys[0], groups).astype(jnp.int32)
        tau = jax.random.permutation(subkeys[1], groups).astype(jnp.int32)
        loads = mean_load + pattern[(sigma[None, :] + tau[:, None]) % groups]
        ends = jnp.cumsum(loads, axis=1)
        begins = ends - loads
        row_index = jnp.arange(TOK_DEV, dtype=jnp.int32)
        target = jnp.sum((ends[:, None, :] <= row_index[None, :, None]).astype(jnp.int32), axis=2)
        within = row_index[None, :] - jnp.take_along_axis(begins, target, axis=1)
        offsets = jnp.cumsum(loads, axis=0) - loads
        place = jnp.take_along_axis(offsets, target, axis=1) + within
        orders = jax.vmap(lambda sub: jax.random.permutation(sub, TOK_DEV))(jax.random.split(subkeys[2], groups)).astype(jnp.int32)
        landing = orders[target, place]
        shuffle = jax.vmap(lambda sub: jax.random.permutation(sub, TOK_DEV))(jax.random.split(subkeys[3], groups)).astype(jnp.int32)
        target = jnp.take_along_axis(target, shuffle, axis=1)
        landing = jnp.take_along_axis(landing, shuffle, axis=1)
        return (target.reshape(-1), landing.reshape(-1))
    return jax.vmap(one_section)(jax.random.split(key, N_SECTION))


def draw_tile_target(key, part):
    return tile_layout(key)[0].astype(jnp.int32)


def draw_tile_row(key, part):
    return tile_layout(key)[1].astype(jnp.int32)


def draw_keys(key, part):
    key = jax.random.fold_in(key, 3)
    drawn = 1.2 * jax.random.truncated_normal(key, -4.0, 4.0, (N_SECTION, TOKENS, ATTN_WIDTH), jnp.float32)
    return drawn.astype(jnp.bfloat16)


def draw_query(key, part):
    key = jax.random.fold_in(key, 7)
    shape_all = (N_SECTION, TOKENS, ATTN_WIDTH)
    drawn = 1.2 * jax.random.truncated_normal(key, -4.0, 4.0, shape_all, jnp.float32)
    return drawn.astype(jnp.bfloat16)


def draw_positions(key, part):
    key = jax.random.fold_in(key, 5)
    ticket = jax.random.randint(key, (N_SECTION, TOKENS), 0, 96)
    row_index = lax.broadcasted_iota(jnp.int32, (N_SECTION, TOKENS), 1)
    later_start = (ticket == 0) & (row_index >= TOK_DEV) & (row_index % 128 != 127)
    begins_here = later_start | (row_index % TOK_DEV == 0)
    latest = lax.cummax(jnp.where(begins_here, row_index, 0), axis=1)
    return (row_index - latest).astype(jnp.int32)


def raised(array, own_key, source, target, shards_of, factor):
    owner, partner = [(jnp.arange(array.shape[axis_at]) // (array.shape[axis_at] // shards_of)).reshape([-1 if axis == axis_at else 1 for axis in range(array.ndim)]) for axis_at in (source, target)]
    chosen = jax.random.permutation(own_key, shards_of)[partner]
    strong = (owner == chosen) | (owner == (partner + shards_of // 2) % shards_of)
    return jnp.where(strong, factor * array, array)


def block_scale(own_key, dims, pieces, least, top_value):
    def one(axis_at, shards_of):
        draws = jax.random.uniform(jax.random.fold_in(jax.random.fold_in(own_key, 6), axis_at), (shards_of,), jnp.float32, least / len(pieces), top_value / len(pieces))
        return jnp.repeat(jnp.exp(draws), dims[axis_at] // shards_of).reshape((-1,) + (1,) * (len(dims) - axis_at - 1))

    level = one(*pieces[0])
    for cut in pieces[1:]:
        level = level * one(*cut)
    return level


def normal_values(stream_key, dims, spread, most, cuts=(), held_as=jnp.bfloat16):
    gain = block_scale(stream_key, dims, cuts, -0.22, 0.18) if cuts else 1.0
    array = jax.random.normal(stream_key, dims, jnp.float32) * spread * gain
    return jnp.minimum(jnp.maximum(array, -most), most).astype(held_as)


def bell_draw_with(own_key, shape, deviation, limit, shards, heavy, kind=jnp.bfloat16):
    array = deviation * jax.random.normal(own_key, shape, jnp.float32)
    if shards:
        array = array * block_scale(own_key, shape, shards, -0.22, 0.18)
    return jnp.clip(raised(array, jax.random.fold_in(own_key, 3), *heavy), -limit, limit).astype(kind)


def setup_inputs(seed: int = 0) -> dict:
    seeds = jax.random.split(jax.random.key(seed), 11)
    return {
        "boundary_grad": normal_values(seeds[0], (N_SECTION, TOKENS, D), 1.0, 6.0, ((0, 2), (1, 16), (2, 4))),
        "tile_target": draw_tile_target(jax.random.fold_in(seeds[10], 71), 0),
        "tile_row": draw_tile_row(jax.random.fold_in(seeds[10], 71), 0),
        "normed_input": bell_draw_with(seeds[3], (N_SECTION, TOKENS, D), 1.0, 6.0, ((0, 2), (1, 16)), (1, 2, 16, 2.0)),
        "query": draw_query(jax.random.fold_in(seeds[10], 71), 0),
        "keys": draw_keys(jax.random.fold_in(seeds[10], 71), 0),
        "values": normal_values(seeds[6], (N_SECTION, TOKENS, ATTN_WIDTH), 1.0, 6.0, ((0, 2), (1, 16), (2, 4))),
        "positions": draw_positions(jax.random.fold_in(seeds[10], 71), 0),
        "out_weight": normal_values(seeds[8], (N_SECTION, D, ATTN_WIDTH), ATTN_WIDTH ** -0.5, 0.09375, ((0, 2), (1, 16), (2, 4))),
        "value_weight": normal_values(seeds[9], (N_SECTION, D, ATTN_WIDTH), D ** -0.5, 0.09375, ((0, 2), (1, 16), (2, 4))),
    }


def rounded(values_in):
    return lax.optimization_barrier(values_in.astype(jnp.bfloat16)).astype(jnp.float32)


def block_backward(operands):
    query_block, key_block, value_block, position_block, gout_block = operands
    tok_rows = query_block.shape[0]
    heads_here = query_block.shape[1] // HEAD_DIM
    scale = HEAD_DIM ** -0.5
    query_heads = query_block.astype(jnp.float32).reshape(tok_rows, heads_here, HEAD_DIM)
    key_heads = key_block.astype(jnp.float32).reshape(tok_rows, heads_here, HEAD_DIM)
    value_heads = value_block.astype(jnp.float32).reshape(tok_rows, heads_here, HEAD_DIM)
    gout_heads = gout_block.astype(jnp.float32).reshape(tok_rows, heads_here, HEAD_DIM)
    row_index = jnp.arange(tok_rows, dtype=jnp.int32)
    allowed = (row_index[None, :] <= row_index[:, None]) & (row_index[None, :] >= (row_index - position_block)[:, None])
    scores = jnp.einsum("qhe,khe->hqk", query_heads, key_heads) * scale
    scores = jnp.where(allowed[None], scores, -1e30)
    highest = jnp.max(scores, axis=-1, keepdims=True)
    weights = jnp.exp(scores - highest)
    probs = weights / jnp.sum(weights, axis=-1, keepdims=True)
    probs_low = rounded(probs)
    attended = jnp.einsum("hqk,khe->qhe", probs_low, value_heads).astype(jnp.bfloat16)
    dprob = jnp.einsum("qhe,khe->hqk", gout_heads, value_heads)
    delta = jnp.sum(probs * dprob, axis=-1, keepdims=True)
    dscore = rounded(probs * (dprob - delta))
    grad_value = jnp.einsum("hqk,qhe->khe", probs_low, gout_heads).astype(jnp.bfloat16)
    grad_query = (jnp.einsum("hqk,khe->qhe", dscore, key_heads) * scale).astype(jnp.bfloat16)
    grad_key = (jnp.einsum("hqk,qhe->khe", dscore, query_heads) * scale).astype(jnp.bfloat16)
    flat_shape = (tok_rows, heads_here * HEAD_DIM)
    return (attended.reshape(flat_shape), grad_value.reshape(flat_shape),
            grad_query.reshape(flat_shape), grad_key.reshape(flat_shape))


def weight_terms(grad_rows, attended, normed_rows, grad_value):
    groups = TOKENS // TOK_DEV

    def accumulate(carry, block_id):
        first_row = block_id * TOK_DEV
        grad_block = lax.dynamic_slice_in_dim(grad_rows, first_row, TOK_DEV, 0)
        attended_block = lax.dynamic_slice_in_dim(attended, first_row, TOK_DEV, 0)
        normed_block = lax.dynamic_slice_in_dim(normed_rows, first_row, TOK_DEV, 0)
        gvalue_block = lax.dynamic_slice_in_dim(grad_value, first_row, TOK_DEV, 0)
        out_term = rounded(jnp.dot(grad_block.T, attended_block, preferred_element_type=jnp.float32))
        value_term = rounded(jnp.dot(normed_block.T, gvalue_block, preferred_element_type=jnp.float32))
        return (carry[0] + out_term, carry[1] + value_term), block_id

    zeros = jnp.zeros((D, ATTN_WIDTH), jnp.float32)
    totals, unused = lax.scan(accumulate, (zeros, zeros), jnp.arange(groups, dtype=jnp.int32))
    return totals


def reference(boundary_grad, tile_target, tile_row, normed_input, query, keys, values, positions, out_weight, value_weight):
    groups = TOKENS // TOK_DEV
    arrived = jnp.zeros_like(boundary_grad)
    for sender in range(N_SECTION):
        row_index = tile_target[sender] * TOK_DEV + tile_row[sender]
        arrived = arrived.at[(sender + 1) % N_SECTION, row_index].set(boundary_grad[sender])
    inputs_out, queries_out, keys_out, outw_out, valw_out = [], [], [], [], []
    cols = ATTN_WIDTH // N_NARROW
    for which in range(N_SECTION):
        grad_rows = arrived[which]
        grad_attended = jnp.dot(grad_rows, out_weight[which], preferred_element_type=jnp.float32).astype(jnp.bfloat16)
        blocked = (query[which].reshape(groups, TOK_DEV, ATTN_WIDTH),
                   keys[which].reshape(groups, TOK_DEV, ATTN_WIDTH),
                   values[which].reshape(groups, TOK_DEV, ATTN_WIDTH),
                   positions[which].reshape(groups, TOK_DEV),
                   grad_attended.reshape(groups, TOK_DEV, ATTN_WIDTH))
        attended, grad_value, grad_query, grad_key = lax.map(block_backward, blocked)
        attended = attended.reshape(TOKENS, ATTN_WIDTH)
        grad_value = grad_value.reshape(TOKENS, ATTN_WIDTH)
        summed = jnp.zeros((TOKENS, D), jnp.float32)
        for group in range(N_NARROW):
            piece = jnp.dot(grad_value[:, group * cols:(group + 1) * cols],
                            value_weight[which][:, group * cols:(group + 1) * cols].T,
                            preferred_element_type=jnp.float32)
            summed = summed + rounded(piece)
        inputs_out.append((grad_rows.astype(jnp.float32) + summed).astype(jnp.bfloat16))
        queries_out.append(grad_query.reshape(TOKENS, ATTN_WIDTH))
        keys_out.append(grad_key.reshape(TOKENS, ATTN_WIDTH))
        out_total, value_total = weight_terms(grad_rows, attended, normed_input[which], grad_value)
        outw_out.append(out_total)
        valw_out.append(value_total)
    return (jnp.stack(inputs_out), jnp.stack(queries_out), jnp.stack(keys_out),
            jnp.stack(outw_out), jnp.stack(valw_out))
```

```python
import functools

import jax
import jax.numpy as jnp
from jax import lax
from jax.experimental import pallas as pl
from jax.experimental.pallas import tpu as pltpu
from jax.sharding import PartitionSpec as P

HEAD_DIM = 128
MESH = pl.DeviceIdType.MESH
SLOTS = 48
PAD = 64


class Place:
    def __init__(self):
        self.s = lax.axis_index("section")
        self.w = lax.axis_index("wide")
        self.n = lax.axis_index("narrow")
        self.core = self.w % 2
        self.y = (self.w // 2) % 2
        self.x = self.w // 4
        self.w_xp = (self.w + 4) % 16
        self.w_xm = (self.w + 12) % 16
        self.w_x2 = (self.w + 8) % 16
        self.w_y = self.w + 2 - 4 * self.y
        self.w_core = self.w + 1 - 2 * self.core
        self.y_xp = (self.w_y + 4) % 16
        self.y_xm = (self.w_y + 12) % 16
        self.y_x2 = (self.w_y + 8) % 16
        self.n_p = (self.n + 1) % 4
        self.n_m = (self.n + 3) % 4
        self.n_2 = (self.n + 2) % 4

    def wide(self, w):
        return (self.s, w, self.n)

    def narrow(self, n):
        return (self.s, self.w, n)


class Links:
    def __init__(self, send_sem, recv_sem):
        self.send_sem, self.recv_sem, self.count, self.sent = send_sem, recv_sem, 0, []

    def put(self, src, dst, device):
        copy = pltpu.make_async_remote_copy(
            src_ref=src,
            dst_ref=dst,
            send_sem=self.send_sem.at[self.count],
            recv_sem=self.recv_sem.at[self.count],
            device_id=device,
            device_id_type=MESH,
        )
        copy.start()
        self.count += 1
        self.sent.append(copy)
        return copy

    def drain(self):
        for copy in self.sent:
            copy.wait_send()


def greet(devices):
    barrier = pltpu.get_barrier_semaphore()
    for device in devices:
        pl.semaphore_signal(barrier, inc=1, device_id=device, device_id_type=MESH)
    return barrier


def gather_wide(at, links, own, full, local_sem):
    half = own.shape[0] // 2
    lower, upper = pl.ds(0, half), pl.ds(half, half)
    third, fourth = pl.ds(half, half // 2), pl.ds(half + half // 2, half // 2)
    xp, xm, yy, cc = (at.wide(w) for w in (at.w_xp, at.w_xm, at.w_y, at.w_core))

    def send(w, device, rows=None):
        ref = full.at[w] if rows is None else full.at[w, rows]
        return links.put(ref, ref, device)

    state = {}

    def first():
        state["own"] = pltpu.make_async_copy(own, full.at[at.w], local_sem)
        state["own"].start()
        state["y"] = links.put(own, full.at[at.w], yy)
        state["xp"] = links.put(own, full.at[at.w], xp)
        state["xm"] = links.put(own, full.at[at.w], xm)
        state["core"] = links.put(own, full.at[at.w], cc)

    def second_y():
        state["y"].wait_recv()
        state["b_p"] = send(at.w_y, xp, upper)
        state["b_m"] = send(at.w_y, xm, upper)
        state["c_y"] = send(at.w_y, cc)

    def second_x():
        state["xp"].wait_recv()
        state["f_p"] = send(at.w_xm, xp, lower)
        state["g_m"] = send(at.w_xm, yy, lower)
        state["c_m"] = send(at.w_xm, cc)
        state["xm"].wait_recv()
        state["f_m"] = send(at.w_xp, xm, upper)
        state["g_p"] = send(at.w_xp, yy, lower)
        state["c_p"] = send(at.w_xp, cc)

    def third_step():
        state["b_p"].wait_recv()
        state["h_p"] = send(at.y_xm, xp, third)
        state["b_m"].wait_recv()
        state["h_m"] = send(at.y_xp, xm, fourth)
        state["f_p"].wait_recv()
        state["g_2"] = send(at.w_x2, yy, lower)
        state["f_m"].wait_recv()
        state["c_2"] = send(at.w_x2, cc)

    def fourth_step():
        state["g_m"].wait_recv()
        state["e_m"] = send(at.y_xm, cc)
        state["g_p"].wait_recv()
        state["e_p"] = send(at.y_xp, cc)
        state["h_p"].wait_recv()
        state["h_m"].wait_recv()
        state["g_2"].wait_recv()
        state["e_2"] = send(at.y_x2, cc)

    def last():
        state["own"].wait()
        for name in ("core", "c_y", "c_m", "c_p", "c_2", "e_m", "e_p", "e_2"):
            state[name].wait_recv()

    return first, second_y, second_x, third_step, fourth_step, last


def relay_kernel(
    tile_ref, target_ref, row_ref, wo_ref, vw_ref,
    g_ref, wo_all, vw_all,
    packed, places, landed, landed_places, spread, canvas, vw_own,
    send_sem, recv_sem, data_send, data_recv, place_send, place_recv, share_send, share_recv, local_sem,
):
    at = Place()
    groups = 16
    tok = tile_ref.shape[0]
    barrier = greet(
        [(1 - at.s, t, at.n) for t in range(groups)]
        + [at.wide(w) for w in (at.w_xp, at.w_xm, at.w_y)]
        + [(at.s, w, n) for w in (at.w, at.w_core) for n in (at.n_p, at.n_m, at.n_2)]
        + [at.wide(at.w_core)]
    )

    target = target_ref[...]
    group = lax.broadcasted_iota(jnp.int32, (groups, tok), 0)
    member = jnp.where(group == target, 1.0, 0.0).astype(jnp.float32)
    before = jnp.where(
        lax.broadcasted_iota(jnp.int32, (tok, tok), 0) < lax.broadcasted_iota(jnp.int32, (tok, tok), 1), 1.0, 0.0
    ).astype(jnp.bfloat16)
    earlier = jnp.dot(member.astype(jnp.bfloat16), before, preferred_element_type=jnp.float32)
    within = jnp.sum(earlier * member, axis=0, keepdims=True).astype(jnp.int32)
    slot = target * SLOTS + within
    choose = jnp.where(
        lax.broadcasted_iota(jnp.int32, (groups * SLOTS, tok), 0) == slot, 1.0, 0.0
    ).astype(jnp.bfloat16)
    packed[...] = jnp.dot(choose, tile_ref[...], preferred_element_type=jnp.float32).astype(jnp.bfloat16)

    lane = within + PAD * (at.w % 2)
    to_lane = jnp.where(
        lax.broadcasted_iota(jnp.int32, (128, tok), 0) == lane, 1.0, 0.0
    ).astype(jnp.bfloat16)
    place = row_ref[...] + 1
    high = (place // 32).astype(jnp.float32)
    low = (place % 32).astype(jnp.float32)
    nt = (((1,), (1,)), ((), ()))
    high = lax.dot_general((member * high).astype(jnp.bfloat16), to_lane, nt, preferred_element_type=jnp.float32)
    low = lax.dot_general((member * low).astype(jnp.bfloat16), to_lane, nt, preferred_element_type=jnp.float32)
    lanes = (high * 32.0 + low).astype(jnp.int32)
    places[...] = jnp.broadcast_to(lanes[:, None, :], places.shape)
    landed[:, SLOTS:, :] = jnp.zeros((groups, PAD - SLOTS, landed.shape[2]), landed.dtype)

    pl.semaphore_wait(barrier, groups + 3 + 6 + 1)

    def relay(i):
        t = (at.w + i) % groups
        device = (1 - at.s, t, at.n)
        data = pltpu.make_async_remote_copy(
            src_ref=packed.at[pl.ds(pl.multiple_of(t * SLOTS, 16), SLOTS)],
            dst_ref=landed.at[at.w, pl.ds(0, SLOTS)],
            send_sem=data_send.at[t],
            recv_sem=data_recv.at[at.w],
            device_id=device,
            device_id_type=MESH,
        )
        where = pltpu.make_async_remote_copy(
            src_ref=places.at[t],
            dst_ref=landed_places.at[at.w],
            send_sem=place_send.at[t],
            recv_sem=place_recv.at[at.w],
            device_id=device,
            device_id_type=MESH,
        )
        return data, where

    @pl.loop(0, groups)
    def _(i):
        data, where = relay(i)
        where.start()
        data.start()

    links = Links(send_sem, recv_sem)
    half_chunk = vw_ref.shape[0] // 4

    def share(h, c):
        w, n = at.w - at.core + c, 2 * at.core + h
        src = vw_ref.at[pl.ds((2 * h + c) * half_chunk, half_chunk)]
        dst = vw_own.at[pl.ds(pl.multiple_of(at.n * half_chunk, half_chunk), half_chunk)]
        mine = (at.core == c) & (at.n == n)
        remote = pltpu.make_async_remote_copy(
            src_ref=src, dst_ref=dst, send_sem=share_send.at[2 * h + c], recv_sem=share_recv.at[at.n],
            device_id=(at.s, w, n), device_id_type=MESH,
        )
        local = pltpu.make_async_copy(src, dst, share_recv.at[at.n])
        return mine, remote, local

    for h in range(2):
        for c in range(2):
            mine, remote, local = share(h, c)

            @pl.when(mine)
            def _():
                local.start()

            @pl.when(jnp.logical_not(mine))
            def _():
                remote.start()

    out_steps = gather_wide(at, links, wo_ref, wo_all, local_sem.at[0])
    value_steps = gather_wide(at, links, vw_own, vw_all, local_sem.at[1])
    out_steps[0]()

    for b in range(4):
        piece = vw_own.at[pl.ds(b * half_chunk, half_chunk)]
        pltpu.make_async_copy(piece, piece, share_recv.at[b]).wait()
    value_steps[0]()
    out_steps[1]()
    out_steps[2]()

    @pl.loop(0, groups)
    def _(i):
        data_piece = landed.at[i, pl.ds(0, SLOTS)]
        pltpu.make_async_copy(data_piece, data_piece, data_recv.at[i]).wait()
        place_piece = landed_places.at[i]
        pltpu.make_async_copy(place_piece, place_piece, place_recv.at[i]).wait()

    arrived = landed_places[...].reshape(groups // 2, 2, 8, 128)
    arrived = (arrived[:, 0] + arrived[:, 1])[:, 0, :]
    token = lax.broadcasted_iota(jnp.int32, (tok, 128), 0) + 1
    for k in range(groups // 2):
        spread[:, k * 128 : (k + 1) * 128] = jnp.where(token == arrived[k : k + 1, :], 1.0, 0.0).astype(jnp.bfloat16)
    rows = landed[...].reshape(groups * PAD, landed.shape[2])
    part = tok // 2
    z_p, z_m, z_local = [], [], []
    for h in range(2):
        span = pl.ds(h * part, part)
        canvas[span, :] = jnp.dot(spread[span, :], rows, preferred_element_type=jnp.float32).astype(jnp.bfloat16)
        z_p.append(links.put(canvas.at[span], g_ref.at[at.n, span], at.narrow(at.n_p)))
        z_m.append(links.put(canvas.at[span], g_ref.at[at.n, span], at.narrow(at.n_m)))
    z_own = pltpu.make_async_copy(canvas, g_ref.at[at.n], local_sem.at[2])
    z_own.start()

    out_steps[3]()
    value_steps[1]()
    value_steps[2]()
    out_steps[4]()

    first, second = pl.ds(0, part), pl.ds(part, part)
    z_p[0].wait_recv()
    ref = g_ref.at[at.n_m, first]
    on_p = links.put(ref, ref, at.narrow(at.n_p))
    z_m[0].wait_recv()
    z_m[1].wait_recv()
    ref = g_ref.at[at.n_p, second]
    on_m = links.put(ref, ref, at.narrow(at.n_m))
    z_p[1].wait_recv()

    value_steps[3]()
    value_steps[4]()
    on_p.wait_recv()
    on_m.wait_recv()
    z_own.wait()
    out_steps[5]()
    value_steps[5]()

    @pl.loop(0, groups)
    def _(i):
        data, where = relay(i)
        data.wait_send()
        where.wait_send()

    for h in range(2):
        for c in range(2):
            mine, remote, local = share(h, c)

            @pl.when(jnp.logical_not(mine))
            def _():
                remote.wait_send()

    links.drain()


def relay_and_gather(tile, target, row, wo, vw):
    tok, width = tile.shape
    bf16 = jnp.bfloat16
    dma = pltpu.SemaphoreType.DMA
    vmem = pl.BlockSpec(memory_space=pltpu.VMEM)
    hbm = pl.BlockSpec(memory_space=pl.ANY)
    copies = 46
    return pl.pallas_call(
        relay_kernel,
        out_shape=(
            jax.ShapeDtypeStruct((4, tok, width), bf16),
            jax.ShapeDtypeStruct((16,) + wo.shape, bf16),
            jax.ShapeDtypeStruct((16,) + vw.shape, bf16),
        ),
        in_specs=[vmem] * 5,
        out_specs=(hbm, hbm, hbm),
        scratch_shapes=[
            pltpu.VMEM((16 * SLOTS, width), bf16),
            pltpu.VMEM((16, 8, 128), jnp.int32),
            pltpu.VMEM((16, PAD, width), bf16),
            pltpu.VMEM((16, 8, 128), jnp.int32),
            pltpu.VMEM((tok, 16 * PAD), bf16),
            pltpu.VMEM((tok, width), bf16),
            pltpu.VMEM(vw.shape, bf16),
            dma((copies,)), dma((copies,)),
            dma((16,)), dma((16,)), dma((16,)), dma((16,)),
            dma((4,)), dma((4,)), dma((3,)),
        ],
        compiler_params=pltpu.CompilerParams(
            collective_id=0, has_side_effects=True, vmem_limit_bytes=40 * 1024 * 1024
        ),
        name="relay_and_gather",
    )(tile, target, row, wo, vw)


def attention_backward(query_rows, key_rows, value_rows, position_rows, grad_attended):
    tok_rows = query_rows.shape[0]
    heads_here = query_rows.shape[1] // HEAD_DIM
    scale = HEAD_DIM ** (-0.5)
    query_heads = query_rows.reshape(tok_rows, heads_here, HEAD_DIM)
    key_heads = key_rows.reshape(tok_rows, heads_here, HEAD_DIM)
    value_heads = value_rows.reshape(tok_rows, heads_here, HEAD_DIM)
    gout_heads = grad_attended.reshape(tok_rows, heads_here, HEAD_DIM)
    index = jnp.arange(tok_rows, dtype=jnp.int32)
    allowed = (index[None, :] <= index[:, None]) & (index[None, :] >= (index - position_rows)[:, None])
    f32 = dict(preferred_element_type=jnp.float32)
    scores = jnp.einsum("qhe,khe->hqk", query_heads, key_heads, **f32) * scale
    scores = jnp.where(allowed[None], scores, -1e30)
    weights = jnp.exp(scores - jnp.max(scores, axis=-1, keepdims=True))
    probs = weights / jnp.sum(weights, axis=-1, keepdims=True)
    probs_low = probs.astype(jnp.bfloat16)
    attended = jnp.einsum("hqk,khe->qhe", probs_low, value_heads, **f32).astype(jnp.bfloat16)
    dprob = jnp.einsum("qhe,khe->hqk", gout_heads, value_heads, **f32)
    delta = jnp.sum(probs * dprob, axis=-1, keepdims=True)
    dscore = (probs * (dprob - delta)).astype(jnp.bfloat16)
    grad_value = jnp.einsum("hqk,qhe->khe", probs_low, gout_heads, **f32).astype(jnp.bfloat16)
    grad_key = (jnp.einsum("hqk,qhe->khe", dscore, query_heads, **f32) * scale).astype(jnp.bfloat16)
    grad_query = (jnp.einsum("hqk,khe->qhe", dscore, key_heads, **f32) * scale).astype(jnp.bfloat16)
    flat = (tok_rows, heads_here * HEAD_DIM)
    return tuple(a.reshape(flat) for a in (attended, grad_value, grad_query, grad_key))


def shards(boundary_grad, tile_target, tile_row, normed_input, query, keys, values, positions, out_weight, value_weight):
    f32 = dict(preferred_element_type=jnp.float32)
    full_grad, out_all, value_all = relay_and_gather(
        boundary_grad[0], tile_target, tile_row, out_weight[0], value_weight[0]
    )
    tok, width = full_grad.shape[1:]
    grad_attended = jnp.einsum("btd,bdh->th", full_grad, out_all.reshape(4, width, width), **f32).astype(jnp.bfloat16)
    attended, grad_value, grad_query, grad_key = attention_backward(
        query[0], keys[0], values[0], positions[0], grad_attended
    )

    def scattered(term):
        return lax.psum_scatter(
            term.astype(jnp.bfloat16), "wide", scatter_dimension=0, tiled=True
        ).astype(jnp.float32)

    out_term = jnp.einsum("btd,th->bdh", full_grad, attended, **f32).reshape(4 * width, width)
    grad_out_weight = scattered(out_term)
    value_term = jnp.einsum("td,th->dh", normed_input[0], grad_value, **f32)
    grad_value_weight = scattered(value_term)
    gv_all = lax.all_gather(grad_value, "narrow", axis=0)
    piece = jnp.einsum("btk,jcbik->tjci", gv_all, value_all.reshape(8, 2, 4, 64, width), **f32).reshape(tok, 8, 128)
    whole = jnp.transpose(full_grad, (1, 0, 2)).reshape(tok, 8, 4, 128)
    mine = lax.dynamic_slice_in_dim(whole, lax.axis_index("narrow"), 1, 2)[:, :, 0]
    piece = (mine.astype(jnp.float32) + piece).astype(jnp.bfloat16)
    grad_input = lax.all_gather(piece, "narrow", axis=2).reshape(tok, 4 * width)
    return (grad_input[None], grad_query[None], grad_key[None], grad_out_weight[None], grad_value_weight[None])


def solution(mesh):
    split = P("section", "wide", "narrow")
    rows = P("section", "wide")
    in_specs = (split, rows, rows, P("section", "wide", None), split, split, split, rows, split, split)
    out_specs = (P("section", "wide", None), split, split, split, split)
    return jax.shard_map(shards, mesh=mesh, in_specs=in_specs, out_specs=out_specs, check_vma=False)
```

```python
import functools

import jax
import jax.numpy as jnp
from jax import lax
from jax.experimental import pallas as pl
from jax.experimental.pallas import tpu as pltpu
from jax.sharding import PartitionSpec as P

HEAD_DIM = 128
MESH = pl.DeviceIdType.MESH
NT = (((1,), (1,)), ((), ()))
TN = (((0,), (0,)), ((), ()))
SLOTS = 48
PAD = 64


class Place:
    def __init__(self):
        self.s = lax.axis_index("section")
        self.w = lax.axis_index("wide")
        self.n = lax.axis_index("narrow")
        self.core = self.w % 2
        self.y = (self.w // 2) % 2
        self.x = self.w // 4
        self.w_xp = (self.w + 4) % 16
        self.w_xm = (self.w + 12) % 16
        self.w_x2 = (self.w + 8) % 16
        self.w_y = self.w + 2 - 4 * self.y
        self.w_core = self.w + 1 - 2 * self.core
        self.y_xp = (self.w_y + 4) % 16
        self.y_xm = (self.w_y + 12) % 16
        self.y_x2 = (self.w_y + 8) % 16
        self.n_p = (self.n + 1) % 4
        self.n_m = (self.n + 3) % 4
        self.n_2 = (self.n + 2) % 4

    def wide(self, w):
        return (self.s, w, self.n)

    def narrow(self, n):
        return (self.s, self.w, n)


class Links:
    def __init__(self, send_sem, recv_sem):
        self.send_sem, self.recv_sem, self.count, self.sent = send_sem, recv_sem, 0, []

    def put(self, src, dst, device):
        copy = pltpu.make_async_remote_copy(
            src_ref=src,
            dst_ref=dst,
            send_sem=self.send_sem.at[self.count],
            recv_sem=self.recv_sem.at[self.count],
            device_id=device,
            device_id_type=MESH,
        )
        copy.start()
        self.count += 1
        self.sent.append(copy)
        return copy

    def drain(self):
        for copy in self.sent:
            copy.wait_send()


def greet(devices):
    barrier = pltpu.get_barrier_semaphore()
    for device in devices:
        pl.semaphore_signal(barrier, inc=1, device_id=device, device_id_type=MESH)
    return barrier


def gather_wide(at, links, own, full, local_sem):
    half = own.shape[0] // 2
    lower, upper = pl.ds(0, half), pl.ds(half, half)
    third, fourth = pl.ds(half, half // 2), pl.ds(half + half // 2, half // 2)
    xp, xm, yy, cc = (at.wide(w) for w in (at.w_xp, at.w_xm, at.w_y, at.w_core))

    def send(w, device, rows=None):
        ref = full.at[w] if rows is None else full.at[w, rows]
        return links.put(ref, ref, device)

    state = {}

    def first():
        state["own"] = pltpu.make_async_copy(own, full.at[at.w], local_sem)
        state["own"].start()
        state["y"] = links.put(own, full.at[at.w], yy)
        state["xp"] = links.put(own, full.at[at.w], xp)
        state["xm"] = links.put(own, full.at[at.w], xm)
        state["core"] = links.put(own, full.at[at.w], cc)

    def second_y():
        state["y"].wait_recv()
        state["b_p"] = send(at.w_y, xp, upper)
        state["b_m"] = send(at.w_y, xm, upper)
        state["c_y"] = send(at.w_y, cc)

    def second_x():
        state["xp"].wait_recv()
        state["f_p"] = send(at.w_xm, xp, lower)
        state["g_m"] = send(at.w_xm, yy, lower)
        state["c_m"] = send(at.w_xm, cc)
        state["xm"].wait_recv()
        state["f_m"] = send(at.w_xp, xm, upper)
        state["g_p"] = send(at.w_xp, yy, lower)
        state["c_p"] = send(at.w_xp, cc)

    def third_step():
        state["b_p"].wait_recv()
        state["h_p"] = send(at.y_xm, xp, third)
        state["b_m"].wait_recv()
        state["h_m"] = send(at.y_xp, xm, fourth)
        state["f_p"].wait_recv()
        state["g_2"] = send(at.w_x2, yy, lower)
        state["f_m"].wait_recv()
        state["c_2"] = send(at.w_x2, cc)

    def fourth_step():
        state["g_m"].wait_recv()
        state["e_m"] = send(at.y_xm, cc)
        state["g_p"].wait_recv()
        state["e_p"] = send(at.y_xp, cc)
        state["h_p"].wait_recv()
        state["h_m"].wait_recv()
        state["g_2"].wait_recv()
        state["e_2"] = send(at.y_x2, cc)

    def last():
        state["own"].wait()
        for name in ("core", "c_y", "c_m", "c_p", "c_2", "e_m", "e_p", "e_2"):
            state[name].wait_recv()

    return first, second_y, second_x, third_step, fourth_step, last


def attention_forward(head, query_ref, key_ref, value_ref, allowed, probs_ref, attended_ref):
    lanes = pl.ds(pl.multiple_of(head * HEAD_DIM, HEAD_DIM), HEAD_DIM)
    scores = lax.dot_general(key_ref[:, lanes], query_ref[:, lanes], NT, preferred_element_type=jnp.float32)
    scores = jnp.where(allowed, scores * HEAD_DIM**-0.5, -1e30)
    weights = jnp.exp(scores - jnp.max(scores, axis=0, keepdims=True))
    probs = (weights / jnp.sum(weights, axis=0, keepdims=True)).astype(jnp.bfloat16)
    probs_ref[head] = probs
    attended = lax.dot_general(probs, value_ref[:, lanes], TN, preferred_element_type=jnp.float32)
    attended_ref[:, lanes] = attended.astype(jnp.bfloat16)


def relay_kernel(
    tile_hbm, target_ref, row_ref, wo_ref, vw_ref, query_hbm, key_hbm, value_hbm, position_ref,
    g_ref, wo_all, vw_all, probs_ref, attended_ref,
    tile_ref, query_ref, key_ref, value_ref, packed, places, landed, landed_places, spread, canvas, vw_own,
    send_sem, recv_sem, data_send, data_recv, place_send, place_recv, share_send, share_recv, local_sem, load_sem,
):
    at = Place()
    loads = [
        pltpu.make_async_copy(src, dst, load_sem.at[k])
        for k, (src, dst) in enumerate(
            ((tile_hbm, tile_ref), (query_hbm, query_ref), (key_hbm, key_ref), (value_hbm, value_ref))
        )
    ]
    for load in loads:
        load.start()
    groups = 16
    tok = tile_ref.shape[0]
    barrier = greet(
        [(1 - at.s, t, at.n) for t in range(groups)]
        + [at.wide(w) for w in (at.w_xp, at.w_xm, at.w_y)]
        + [(at.s, w, n) for w in (at.w, at.w_core) for n in (at.n_p, at.n_m, at.n_2)]
        + [at.wide(at.w_core)]
    )

    target = target_ref[...]
    group = lax.broadcasted_iota(jnp.int32, (groups, tok), 0)
    member = jnp.where(group == target, 1.0, 0.0).astype(jnp.float32)
    before = jnp.where(
        lax.broadcasted_iota(jnp.int32, (tok, tok), 0) < lax.broadcasted_iota(jnp.int32, (tok, tok), 1), 1.0, 0.0
    ).astype(jnp.bfloat16)
    earlier = jnp.dot(member.astype(jnp.bfloat16), before, preferred_element_type=jnp.float32)
    within = jnp.sum(earlier * member, axis=0, keepdims=True).astype(jnp.int32)
    slot = target * SLOTS + within
    choose = jnp.where(
        lax.broadcasted_iota(jnp.int32, (groups * SLOTS, tok), 0) == slot, 1.0, 0.0
    ).astype(jnp.bfloat16)
    loads[0].wait()
    packed[...] = jnp.dot(choose, tile_ref[...], preferred_element_type=jnp.float32).astype(jnp.bfloat16)

    lane = within + PAD * (at.w % 2)
    to_lane = jnp.where(
        lax.broadcasted_iota(jnp.int32, (128, tok), 0) == lane, 1.0, 0.0
    ).astype(jnp.bfloat16)
    place = row_ref[...] + 1
    high = (place // 32).astype(jnp.float32)
    low = (place % 32).astype(jnp.float32)
    high = lax.dot_general((member * high).astype(jnp.bfloat16), to_lane, NT, preferred_element_type=jnp.float32)
    low = lax.dot_general((member * low).astype(jnp.bfloat16), to_lane, NT, preferred_element_type=jnp.float32)
    lanes = (high * 32.0 + low).astype(jnp.int32)
    places[...] = jnp.broadcast_to(lanes[:, None, :], places.shape)
    landed[:, SLOTS:, :] = jnp.zeros((groups, PAD - SLOTS, landed.shape[2]), landed.dtype)

    pl.semaphore_wait(barrier, groups + 3 + 6 + 1)

    def relay(i):
        t = (at.w + i) % groups
        device = (1 - at.s, t, at.n)
        data = pltpu.make_async_remote_copy(
            src_ref=packed.at[pl.ds(pl.multiple_of(t * SLOTS, 16), SLOTS)],
            dst_ref=landed.at[at.w, pl.ds(0, SLOTS)],
            send_sem=data_send.at[t],
            recv_sem=data_recv.at[at.w],
            device_id=device,
            device_id_type=MESH,
        )
        where = pltpu.make_async_remote_copy(
            src_ref=places.at[t],
            dst_ref=landed_places.at[at.w],
            send_sem=place_send.at[t],
            recv_sem=place_recv.at[at.w],
            device_id=device,
            device_id_type=MESH,
        )
        return data, where

    @pl.loop(0, groups)
    def _(i):
        data, where = relay(i)
        where.start()
        data.start()

    links = Links(send_sem, recv_sem)
    half_chunk = vw_ref.shape[0] // 4

    def share(h, c):
        w, n = at.w - at.core + c, 2 * at.core + h
        src = vw_ref.at[pl.ds((2 * h + c) * half_chunk, half_chunk)]
        dst = vw_own.at[pl.ds(pl.multiple_of(at.n * half_chunk, half_chunk), half_chunk)]
        mine = (at.core == c) & (at.n == n)
        remote = pltpu.make_async_remote_copy(
            src_ref=src, dst_ref=dst, send_sem=share_send.at[2 * h + c], recv_sem=share_recv.at[at.n],
            device_id=(at.s, w, n), device_id_type=MESH,
        )
        local = pltpu.make_async_copy(src, dst, share_recv.at[at.n])
        return mine, remote, local

    for h in range(2):
        for c in range(2):
            mine, remote, local = share(h, c)

            @pl.when(mine)
            def _():
                local.start()

            @pl.when(jnp.logical_not(mine))
            def _():
                remote.start()

    out_steps = gather_wide(at, links, wo_ref, wo_all, local_sem.at[0])
    value_steps = gather_wide(at, links, vw_own, vw_all, local_sem.at[1])
    out_steps[0]()

    key_at = lax.broadcasted_iota(jnp.int32, (tok, tok), 0)
    query_at = lax.broadcasted_iota(jnp.int32, (tok, tok), 1)
    earliest = lax.broadcasted_iota(jnp.int32, (1, tok), 1) - position_ref[...]

    def heads(first, last):
        @pl.loop(first, last)
        def _(head):
            allowed = (key_at <= query_at) & (key_at >= earliest)
            attention_forward(head, query_ref, key_ref, value_ref, allowed, probs_ref, attended_ref)

    for load in loads[1:]:
        load.wait()
    heads(0, 2)

    for b in range(4):
        piece = vw_own.at[pl.ds(b * half_chunk, half_chunk)]
        pltpu.make_async_copy(piece, piece, share_recv.at[b]).wait()
    value_steps[0]()
    out_steps[1]()
    out_steps[2]()
    heads(2, 5)

    @pl.loop(0, groups)
    def _(i):
        data_piece = landed.at[i, pl.ds(0, SLOTS)]
        pltpu.make_async_copy(data_piece, data_piece, data_recv.at[i]).wait()
        place_piece = landed_places.at[i]
        pltpu.make_async_copy(place_piece, place_piece, place_recv.at[i]).wait()

    arrived = landed_places[...].reshape(groups // 2, 2, 8, 128)
    arrived = (arrived[:, 0] + arrived[:, 1])[:, 0, :]
    token = lax.broadcasted_iota(jnp.int32, (tok, 128), 0) + 1
    for k in range(groups // 2):
        spread[:, k * 128 : (k + 1) * 128] = jnp.where(token == arrived[k : k + 1, :], 1.0, 0.0).astype(jnp.bfloat16)
    rows = landed[...].reshape(groups * PAD, landed.shape[2])
    part = tok // 2
    z_p, z_m, z_local = [], [], []
    for h in range(2):
        span = pl.ds(h * part, part)
        canvas[span, :] = jnp.dot(spread[span, :], rows, preferred_element_type=jnp.float32).astype(jnp.bfloat16)
        z_p.append(links.put(canvas.at[span], g_ref.at[at.n, span], at.narrow(at.n_p)))
        z_m.append(links.put(canvas.at[span], g_ref.at[at.n, span], at.narrow(at.n_m)))
    z_own = pltpu.make_async_copy(canvas, g_ref.at[at.n], local_sem.at[2])
    z_own.start()

    out_steps[3]()
    value_steps[1]()
    value_steps[2]()
    out_steps[4]()
    heads(5, 8)

    first, second = pl.ds(0, part), pl.ds(part, part)
    z_p[0].wait_recv()
    ref = g_ref.at[at.n_m, first]
    on_p = links.put(ref, ref, at.narrow(at.n_p))
    z_m[0].wait_recv()
    z_m[1].wait_recv()
    ref = g_ref.at[at.n_p, second]
    on_m = links.put(ref, ref, at.narrow(at.n_m))
    z_p[1].wait_recv()

    value_steps[3]()
    value_steps[4]()
    on_p.wait_recv()
    on_m.wait_recv()
    z_own.wait()
    out_steps[5]()
    value_steps[5]()

    @pl.loop(0, groups)
    def _(i):
        data, where = relay(i)
        data.wait_send()
        where.wait_send()

    for h in range(2):
        for c in range(2):
            mine, remote, local = share(h, c)

            @pl.when(jnp.logical_not(mine))
            def _():
                remote.wait_send()

    links.drain()


def relay_and_gather(tile, target, row, wo, vw, query, key, value, position):
    tok, width = tile.shape
    bf16 = jnp.bfloat16
    dma = pltpu.SemaphoreType.DMA
    vmem = pl.BlockSpec(memory_space=pltpu.VMEM)
    hbm = pl.BlockSpec(memory_space=pl.ANY)
    copies = 46
    return pl.pallas_call(
        relay_kernel,
        out_shape=(
            jax.ShapeDtypeStruct((4, tok, width), bf16),
            jax.ShapeDtypeStruct((16,) + wo.shape, bf16),
            jax.ShapeDtypeStruct((16,) + vw.shape, bf16),
            jax.ShapeDtypeStruct((width // HEAD_DIM, tok, tok), bf16),
            jax.ShapeDtypeStruct((tok, width), bf16),
        ),
        in_specs=[hbm, vmem, vmem, hbm, hbm, hbm, hbm, hbm, vmem],
        out_specs=(hbm, hbm, hbm, vmem, vmem),
        scratch_shapes=[
            *[pltpu.VMEM((tok, width), bf16)] * 4,
            pltpu.VMEM((16 * SLOTS, width), bf16),
            pltpu.VMEM((16, 8, 128), jnp.int32),
            pltpu.VMEM((16, PAD, width), bf16),
            pltpu.VMEM((16, 8, 128), jnp.int32),
            pltpu.VMEM((tok, 16 * PAD), bf16),
            pltpu.VMEM((tok, width), bf16),
            pltpu.VMEM(vw.shape, bf16),
            dma((copies,)), dma((copies,)),
            dma((16,)), dma((16,)), dma((16,)), dma((16,)),
            dma((4,)), dma((4,)), dma((3,)), dma((4,)),
        ],
        compiler_params=pltpu.CompilerParams(
            collective_id=0, has_side_effects=True, vmem_limit_bytes=60 * 1024 * 1024
        ),
        name="relay_and_gather",
    )(tile, target, row, wo, vw, query, key, value, position)


def scatter_wide(at, links, mine, from_y, via, from_x, result):
    half = result.shape[0] // 2
    quarter = half // 2
    lower, upper = pl.ds(0, half), pl.ds(half, half)
    xp, xm, yy = (at.wide(w) for w in (at.w_xp, at.w_xm, at.w_y))
    ya, yb = from_y
    state = {}

    def add(dx, dy, rows, *others):
        ref = mine(dx, dy).at[rows]
        total = ref[...].astype(jnp.float32)
        for other in others:
            total = total + other[...].astype(jnp.float32)
        return ref, total

    def add_into(dx, dy, rows, *others):
        ref, total = add(dx, dy, rows, *others)
        ref[...] = total.astype(jnp.bfloat16)

    def across(name, slot, dx_dy, start):
        for k, device in ((0, xp), (1, xm)):
            rows = pl.ds(start + k * quarter, quarter)
            state[name, k] = links.put(mine(*dx_dy).at[rows], via.at[slot, k], device)

    def first_a():
        state["ya2"] = links.put(mine(2, 1).at[lower], ya.at[2], yy)
        across("vb1", 1, (2, 1), half)
        across("vb0", 0, (2, 0), half)

    def first_b():
        for dx in (1, 3, 0):
            state["ya%d" % dx] = links.put(mine(dx, 1).at[lower], ya.at[dx], yy)

    def onward(name, slot, dy, start, rows):
        for k, dx, device in ((0, 1, xp), (1, 3, xm)):
            state[name, k].wait_recv()
            add_into(dx, dy, pl.ds(start + k * quarter, quarter), via.at[slot, k])
            state["r" + name, k] = links.put(mine(dx, dy).at[rows], from_x.at[slot, k], device)

    def second():
        state["ya2"].wait_recv()
        add_into(2, 0, lower, ya.at[2])
        across("va", 2, (2, 0), 0)
        onward("vb1", 1, 1, half, upper)
        onward("vb0", 0, 0, half, upper)

    def third():
        for dx in (1, 3):
            state["ya%d" % dx].wait_recv()
            add_into(dx, 0, lower, ya.at[dx])
        onward("va", 2, 0, 0, lower)
        for k in range(2):
            state["rvb1", k].wait_recv()
        add_into(0, 1, upper, from_x.at[1, 0], from_x.at[1, 1])
        state["yb"] = links.put(mine(0, 1).at[upper], yb, yy)

    def fourth():
        state["ya0"].wait_recv()
        for k in range(2):
            state["rva", k].wait_recv()
        result[lower, :] = add(0, 0, lower, ya.at[0], from_x.at[2, 0], from_x.at[2, 1])[1]
        for k in range(2):
            state["rvb0", k].wait_recv()
        state["yb"].wait_recv()
        result[upper, :] = add(0, 0, upper, yb, from_x.at[0, 0], from_x.at[0, 1])[1]

    return first_a, first_b, second, third, fourth


def backward_kernel(
    g_hbm, attended_hbm, query_hbm, key_hbm, value_hbm, wo_hbm, vw_hbm, probs_hbm, normed_hbm,
    gin_hbm, gq_ref, gk_ref, gow_ref, gvw_ref,
    g_ref, attended_ref, query_ref, key_ref, value_ref, weight, other, out_mine, core_out, core_value, ya_out, yb_out, via_out, x_out, ya_val, yb_val, via_val, x_val,
    gv_own, gv_all, probs, vw_tiles, stage,
    send_sem, recv_sem, core_send, core_recv, gv_send, gv_recv, gin_send, gin_recv, local_sem, probs_sem, tile_sem, own_sem, g_sem,
):
    at = Place()
    tok, width = attended_hbm.shape
    rows = gow_ref.shape[0]
    links = Links(send_sem, recv_sem)
    barrier = greet(
        [at.wide(w) for w in (at.w_xp, at.w_xm, at.w_y, at.w_core)] + [at.narrow(n) for n in (at.n_p, at.n_m)]
    )
    load_g = [
        pltpu.make_async_copy(g_hbm.at[pl.ds(b, 1)], g_ref.at[pl.ds(b, 1)], g_sem.at[b]) for b in range(4)
    ]
    load_g.append(pltpu.make_async_copy(attended_hbm, attended_ref, g_sem.at[4]))
    for load in load_g:
        load.start()
    load_rest = [
        pltpu.make_async_copy(src, dst, local_sem.at[k])
        for k, (src, dst) in enumerate(
            ((query_hbm, query_ref), (key_hbm, key_ref), (value_hbm, value_ref), (wo_hbm, weight))
        )
    ]
    for load in load_rest:
        load.start()

    def load_probs(pair):
        return pltpu.make_async_copy(probs_hbm.at[pl.ds(2 * pair, 2)], probs.at[pair % 2], probs_sem.at[pair % 2])

    load_probs(0).start()

    def chip(dx, dy):
        y = at.y if dy == 0 else 1 - at.y
        return ((at.x + dx) % 4) * 2 + y

    def chip_of(i):
        dx = (2 + i // 2) % 4
        y = (at.y + 1 + i) % 2
        return (at.x + dx) % 4, y

    pl.semaphore_wait(barrier, 6)

    def terms(which, left, right, to_core, mine, landing):
        def send(i):
            x, y = chip_of(i)
            return pltpu.make_async_remote_copy(
                src_ref=to_core(x, y), dst_ref=landing.at[x * 2 + y],
                send_sem=core_send.at[which, i], recv_sem=core_recv.at[which, i],
                device_id=at.wide(at.w_core), device_id_type=MESH,
            )

        def theirs():
            @pl.loop(0, 8)
            def _(i):
                x, y = chip_of(i)
                term = lax.dot_general(left(x, y, 1 - at.core), right[...], TN, preferred_element_type=jnp.float32)
                to_core(x, y)[...] = term.astype(jnp.bfloat16)
                send(i).start()

        def ours(first, last):
            @pl.loop(first, last)
            def _(i):
                x, y = chip_of(i)
                term = lax.dot_general(left(x, y, at.core), right[...], TN, preferred_element_type=jnp.float32)
                send(i).wait_recv()
                term = term + landing[x * 2 + y].astype(jnp.float32)
                mine(x * 2 + y)[...] = term.astype(jnp.bfloat16)

        def drain():
            @pl.loop(0, 8)
            def _(i):
                send(i).wait_send()

        return theirs, ours, drain

    def g_columns(x, y, core):
        return g_ref[x, :, pl.ds(pl.multiple_of(y * 512 + core * 256, 256), 256)]

    def normed_columns(x, y, core):
        return other[:, pl.ds(pl.multiple_of(x * 1024 + y * 512 + core * 256, 256), 256)]

    def in_other(x, y):
        return other.at[pl.ds(pl.multiple_of(y * 256, 256), 256), pl.ds(pl.multiple_of(x * 1024, 1024), 1024)]

    theirs, ours, drain_core = terms(0, g_columns, attended_ref, in_other, lambda j: out_mine.at[j], core_out)
    out_steps = scatter_wide(
        at, links, lambda dx, dy: out_mine.at[chip(dx, dy)], (ya_out, yb_out), via_out, x_out, gow_ref
    )
    for load in load_g:
        load.wait()
    theirs()
    ours(0, 2)
    out_steps[0]()
    ours(2, 8)
    out_steps[1]()
    drain_core()
    load_normed = pltpu.make_async_copy(normed_hbm, other, local_sem.at[4])
    load_normed.start()
    for load in load_rest:
        load.wait()

    part = tok // 2
    scale = HEAD_DIM**-0.5

    def gv_copies(pair):
        def copy(k, src, device):
            return pltpu.make_async_remote_copy(
                src_ref=src, dst_ref=src, send_sem=gv_send.at[k, pair], recv_sem=gv_recv.at[k, pair],
                device_id=at.narrow(device), device_id_type=MESH,
            )

        mine = gv_all.at[at.n, pair]
        on_p = gv_all.at[at.n_m, pair, pl.ds(0, part)]
        on_m = gv_all.at[at.n_p, pair, pl.ds(part, part)]
        return copy(0, mine, at.n_p), copy(1, mine, at.n_m), copy(2, on_p, at.n_p), copy(3, on_m, at.n_m)

    def forward_gv(pair):
        to_p, to_m, on_p, on_m = gv_copies(pair)
        to_p.wait_recv()
        on_p.start()
        to_m.wait_recv()
        on_m.start()

    def attend(pair):
        lanes = pl.ds(pair * 256, 256)
        load_probs(pair).wait()
        if pair < 3:
            load_probs(pair + 1).start()
        total = jnp.zeros((tok, 256), jnp.float32)
        for b in range(4):
            block = weight[4 * b : 4 * b + 4, :, lanes].reshape(width, 256)
            total = total + jnp.dot(g_ref[b], block, preferred_element_type=jnp.float32)
        both = total.astype(jnp.bfloat16)
        for h in range(2):
            cols = pl.ds(pair * 256 + h * HEAD_DIM, HEAD_DIM)
            gout = both[:, h * HEAD_DIM : (h + 1) * HEAD_DIM]
            prob = probs[pair % 2, h]
            dprob = lax.dot_general(value_ref[:, cols], gout, NT, preferred_element_type=jnp.float32)
            wide_prob = prob.astype(jnp.float32)
            delta = jnp.sum(wide_prob * dprob, axis=0, keepdims=True)
            dscore = (wide_prob * (dprob - delta)).astype(jnp.bfloat16)
            gv = jnp.dot(prob, gout, preferred_element_type=jnp.float32).astype(jnp.bfloat16)
            gv_own[:, cols] = gv
            gv_all[at.n, pair, :, pl.ds(h * HEAD_DIM, HEAD_DIM)] = gv
            gk = jnp.dot(dscore, query_ref[:, cols], preferred_element_type=jnp.float32) * scale
            gk_ref[:, cols] = gk.astype(jnp.bfloat16)
            gq = lax.dot_general(dscore, key_ref[:, cols], TN, preferred_element_type=jnp.float32) * scale
            gq_ref[:, cols] = gq.astype(jnp.bfloat16)
        to_p, to_m, _, _ = gv_copies(pair)
        to_p.start()
        to_m.start()
        if pair > 0:
            forward_gv(pair - 1)

    attend(0)
    attend(1)
    out_steps[2]()
    attend(2)
    attend(3)
    out_steps[3]()

    def load_tile(tile):
        return pltpu.make_async_copy(vw_hbm.at[pl.ds(4 * tile, 4)], vw_tiles.at[tile % 2], tile_sem.at[tile % 2])

    load_tile(0).start()
    load_tile(1).start()
    load_normed.wait()
    theirs, ours, drain_value = terms(
        1, normed_columns, gv_own, lambda x, y: weight.at[x * 2 + y], lambda j: weight.at[8 + j], core_value
    )
    value_steps = scatter_wide(
        at, links, lambda dx, dy: weight.at[8 + chip(dx, dy)], (ya_val, yb_val), via_val, x_val, gvw_ref
    )
    theirs()
    forward_gv(3)
    ours(0, 2)
    value_steps[0]()
    ours(2, 8)
    value_steps[1]()

    for pair in range(4):
        _, _, on_p, on_m = gv_copies(pair)
        on_p.wait_recv()
        on_m.wait_recv()

    def gin_copies(tile, y):
        def copy(k, src, dst, device):
            return pltpu.make_async_remote_copy(
                src_ref=src, dst_ref=dst, send_sem=gin_send.at[k, 2 * tile + y], recv_sem=gin_recv.at[k, 2 * tile + y],
                device_id=at.narrow(device), device_id_type=MESH,
            )

        def chunk(n, start, size):
            cols = pl.ds(pl.multiple_of(tile * 1024 + y * 512 + n * 128, 128), 128)
            return gin_hbm.at[pl.ds(start, size), cols]

        src, dst = stage.at[tile, :, pl.ds(y * 128, 128)], chunk(at.n, 0, tok)
        on_p, on_m = chunk(at.n_m, 0, part), chunk(at.n_p, part, part)
        own = pltpu.make_async_copy(src, dst, own_sem.at[2 * tile + y])
        return copy(0, src, dst, at.n_p), copy(1, src, dst, at.n_m), copy(2, on_p, on_p, at.n_p), copy(3, on_m, on_m, at.n_m), own

    def forward_gin(tile):
        for y in range(2):
            to_p, to_m, on_p, on_m, _ = gin_copies(tile, y)
            to_p.wait_recv()
            on_p.start()
            to_m.wait_recv()
            on_m.start()

    for tile in range(4):
        load_tile(tile).wait()
        chunk = pl.multiple_of(at.n * 128, 128)
        low = g_ref[tile, :, pl.ds(chunk, 128)]
        high = g_ref[tile, :, pl.ds(pl.multiple_of(chunk + 512, 128), 128)]
        total = jnp.concatenate([low, high], axis=1).astype(jnp.float32)
        for z in range(4):
            for pair in range(4):
                block = vw_tiles[tile % 2, :, z * 64 : (z + 1) * 64, pair * 256 : (pair + 1) * 256].reshape(256, 256)
                total = total + lax.dot_general(gv_all[z, pair], block, NT, preferred_element_type=jnp.float32)
        stage[tile] = total.astype(jnp.bfloat16)
        for y in range(2):
            to_p, to_m, _, _, own = gin_copies(tile, y)
            to_p.start()
            to_m.start()
            own.start()
        if tile < 2:
            load_tile(tile + 2).start()

    out_steps[4]()
    value_steps[2]()
    forward_gin(0)
    forward_gin(1)
    value_steps[3]()
    forward_gin(2)
    forward_gin(3)
    value_steps[4]()
    drain_value()
    for tile in range(4):
        for y in range(2):
            to_p, to_m, on_p, on_m, own = gin_copies(tile, y)
            on_p.wait_recv()
            on_m.wait_recv()
            own.wait()
            for copy in (to_p, to_m, on_p, on_m):
                copy.wait_send()
        for copy in gv_copies(tile):
            copy.wait_send()
    links.drain()


def backward_and_scatter(full_grad, attended, query, key, value, out_all, value_all, probs, normed):
    _, tok, width = full_grad.shape
    rows = out_all.shape[1]
    bf16, f32 = jnp.bfloat16, jnp.float32
    dma = pltpu.SemaphoreType.DMA
    vmem = pl.BlockSpec(memory_space=pltpu.VMEM)
    hbm = pl.BlockSpec(memory_space=pl.ANY)
    half = rows // 2
    landing = [
        pltpu.VMEM((4, half, width), bf16),
        pltpu.VMEM((half, width), bf16),
        pltpu.VMEM((3, 2, half // 2, width), bf16),
        pltpu.VMEM((3, 2, half, width), bf16),
    ]
    copies = 34
    return pl.pallas_call(
        backward_kernel,
        out_shape=(
            jax.ShapeDtypeStruct((tok, 4 * width), bf16),
            jax.ShapeDtypeStruct((tok, width), bf16),
            jax.ShapeDtypeStruct((tok, width), bf16),
            jax.ShapeDtypeStruct((rows, width), f32),
            jax.ShapeDtypeStruct((rows, width), f32),
        ),
        in_specs=[hbm] * 9,
        out_specs=(hbm, vmem, vmem, vmem, vmem),
        scratch_shapes=[
            pltpu.VMEM((4, tok, width), bf16),
            *[pltpu.VMEM((tok, width), bf16)] * 4,
            pltpu.VMEM((16, rows, width), bf16),
            pltpu.VMEM((tok, 4 * width), bf16),
            pltpu.VMEM((8, rows, width), bf16),
            pltpu.VMEM((8, rows, width), bf16),
            pltpu.VMEM((8, rows, width), bf16),
            *landing,
            *landing,
            pltpu.VMEM((tok, width), bf16),
            pltpu.VMEM((4, 4, tok, 256), bf16),
            pltpu.VMEM((2, 2, tok, tok), bf16),
            pltpu.VMEM((2, 4, rows, width), bf16),
            pltpu.VMEM((4, tok, 256), bf16),
            dma((copies,)), dma((copies,)),
            dma((2, 8)), dma((2, 8)),
            dma((4, 4)), dma((4, 4)), dma((4, 8)), dma((4, 8)),
            dma((5,)), dma((2,)), dma((2,)), dma((8,)), dma((5,)),
        ],
        compiler_params=pltpu.CompilerParams(
            collective_id=1, has_side_effects=True, vmem_limit_bytes=62 * 1024 * 1024
        ),
        name="backward_and_scatter",
    )(full_grad, attended, query, key, value, out_all, value_all, probs, normed)


def shards(boundary_grad, tile_target, tile_row, normed_input, query, keys, values, positions, out_weight, value_weight):
    full_grad, out_all, value_all, probs, attended = relay_and_gather(
        boundary_grad[0], tile_target, tile_row, out_weight[0], value_weight[0], query[0], keys[0], values[0], positions
    )
    grad_input, grad_query, grad_key, grad_out_weight, grad_value_weight = backward_and_scatter(
        full_grad, attended, query[0], keys[0], values[0], out_all, value_all, probs, normed_input[0]
    )
    return (grad_input[None], grad_query[None], grad_key[None], grad_out_weight[None], grad_value_weight[None])


def solution(mesh):
    split = P("section", "wide", "narrow")
    rows = P("section", "wide")
    in_specs = (split, rows, rows, P("section", "wide", None), split, split, split, rows, split, split)
    out_specs = (P("section", "wide", None), split, split, split, split)
    return jax.shard_map(shards, mesh=mesh, in_specs=in_specs, out_specs=out_specs, check_vma=False)
```

```python
import functools

import jax
import jax.numpy as jnp
from jax import lax
from jax.experimental import pallas as pl
from jax.experimental.pallas import tpu as pltpu
from jax.sharding import PartitionSpec as P

HEAD_DIM = 128
MESH = pl.DeviceIdType.MESH
NT = (((1,), (1,)), ((), ()))
TN = (((0,), (0,)), ((), ()))
SLOTS = 48
PAD = 64


class Place:
    def __init__(self):
        self.s = lax.axis_index("section")
        self.w = lax.axis_index("wide")
        self.n = lax.axis_index("narrow")
        self.core = self.w % 2
        self.y = (self.w // 2) % 2
        self.x = self.w // 4
        self.w_xp = (self.w + 4) % 16
        self.w_xm = (self.w + 12) % 16
        self.w_x2 = (self.w + 8) % 16
        self.w_y = self.w + 2 - 4 * self.y
        self.w_core = self.w + 1 - 2 * self.core
        self.y_xp = (self.w_y + 4) % 16
        self.y_xm = (self.w_y + 12) % 16
        self.y_x2 = (self.w_y + 8) % 16
        self.n_p = (self.n + 1) % 4
        self.n_m = (self.n + 3) % 4
        self.n_2 = (self.n + 2) % 4

    def wide(self, w):
        return (self.s, w, self.n)

    def narrow(self, n):
        return (self.s, self.w, n)


class Links:
    def __init__(self, send_sem, recv_sem):
        self.send_sem, self.recv_sem, self.count, self.sent = send_sem, recv_sem, 0, []

    def put(self, src, dst, device):
        copy = pltpu.make_async_remote_copy(
            src_ref=src,
            dst_ref=dst,
            send_sem=self.send_sem.at[self.count],
            recv_sem=self.recv_sem.at[self.count],
            device_id=device,
            device_id_type=MESH,
        )
        copy.start()
        self.count += 1
        self.sent.append(copy)
        return copy

    def drain(self):
        for copy in self.sent:
            copy.wait_send()


def greet(devices):
    barrier = pltpu.get_barrier_semaphore()
    for device in devices:
        pl.semaphore_signal(barrier, inc=1, device_id=device, device_id_type=MESH)
    return barrier


def gather_wide(at, links, own, full, local_sem):
    half = own.shape[0] // 2
    lower, upper = pl.ds(0, half), pl.ds(half, half)
    third, fourth = pl.ds(half, half // 2), pl.ds(half + half // 2, half // 2)
    xp, xm, yy, cc = (at.wide(w) for w in (at.w_xp, at.w_xm, at.w_y, at.w_core))

    def send(w, device, rows=None):
        ref = full.at[w] if rows is None else full.at[w, rows]
        return links.put(ref, ref, device)

    state = {}

    def first():
        state["own"] = pltpu.make_async_copy(own, full.at[at.w], local_sem)
        state["own"].start()
        state["y"] = links.put(own, full.at[at.w], yy)
        state["xp"] = links.put(own, full.at[at.w], xp)
        state["xm"] = links.put(own, full.at[at.w], xm)
        state["core"] = links.put(own, full.at[at.w], cc)

    def second_y():
        state["y"].wait_recv()
        state["b_p"] = send(at.w_y, xp, upper)
        state["b_m"] = send(at.w_y, xm, upper)
        state["c_y"] = send(at.w_y, cc)

    def second_x():
        state["xp"].wait_recv()
        state["f_p"] = send(at.w_xm, xp, lower)
        state["g_m"] = send(at.w_xm, yy, lower)
        state["c_m"] = send(at.w_xm, cc)
        state["xm"].wait_recv()
        state["f_m"] = send(at.w_xp, xm, upper)
        state["g_p"] = send(at.w_xp, yy, lower)
        state["c_p"] = send(at.w_xp, cc)

    def third_step():
        state["b_p"].wait_recv()
        state["h_p"] = send(at.y_xm, xp, third)
        state["b_m"].wait_recv()
        state["h_m"] = send(at.y_xp, xm, fourth)
        state["f_p"].wait_recv()
        state["g_2"] = send(at.w_x2, yy, lower)
        state["f_m"].wait_recv()
        state["c_2"] = send(at.w_x2, cc)

    def fourth_step():
        state["g_m"].wait_recv()
        state["e_m"] = send(at.y_xm, cc)
        state["g_p"].wait_recv()
        state["e_p"] = send(at.y_xp, cc)
        state["h_p"].wait_recv()
        state["h_m"].wait_recv()
        state["g_2"].wait_recv()
        state["e_2"] = send(at.y_x2, cc)

    def last():
        state["own"].wait()
        for name in ("core", "c_y", "c_m", "c_p", "c_2", "e_m", "e_p", "e_2"):
            state[name].wait_recv()

    return first, second_y, second_x, third_step, fourth_step, last


def attention_forward(head, query_ref, key_ref, value_ref, allowed, probs_ref, attended_ref):
    lanes = pl.ds(pl.multiple_of(head * HEAD_DIM, HEAD_DIM), HEAD_DIM)
    scores = lax.dot_general(key_ref[:, lanes], query_ref[:, lanes], NT, preferred_element_type=jnp.float32)
    scores = jnp.where(allowed, scores * HEAD_DIM**-0.5, -1e30)
    weights = jnp.exp(scores - jnp.max(scores, axis=0, keepdims=True))
    probs = (weights / jnp.sum(weights, axis=0, keepdims=True)).astype(jnp.bfloat16)
    probs_ref[head] = probs
    attended = lax.dot_general(probs, value_ref[:, lanes], TN, preferred_element_type=jnp.float32)
    attended_ref[:, lanes] = attended.astype(jnp.bfloat16)


def scatter_wide(at, links, mine, from_y, via, from_x, result):
    half = result.shape[0] // 2
    quarter = half // 2
    lower, upper = pl.ds(0, half), pl.ds(half, half)
    xp, xm, yy = (at.wide(w) for w in (at.w_xp, at.w_xm, at.w_y))
    ya, yb = from_y
    state = {}

    def add(dx, dy, rows, *others):
        ref = mine(dx, dy).at[rows]
        total = ref[...].astype(jnp.float32)
        for other in others:
            total = total + other[...].astype(jnp.float32)
        return ref, total

    def add_into(dx, dy, rows, *others):
        ref, total = add(dx, dy, rows, *others)
        ref[...] = total.astype(jnp.bfloat16)

    def across(name, slot, dx_dy, start):
        for k, device in ((0, xp), (1, xm)):
            rows = pl.ds(start + k * quarter, quarter)
            state[name, k] = links.put(mine(*dx_dy).at[rows], via.at[slot, k], device)

    def first_a():
        state["ya2"] = links.put(mine(2, 1).at[lower], ya.at[2], yy)
        across("vb1", 1, (2, 1), half)
        across("vb0", 0, (2, 0), half)

    def first_b():
        for dx in (1, 3, 0):
            state["ya%d" % dx] = links.put(mine(dx, 1).at[lower], ya.at[dx], yy)

    def onward(name, slot, dy, start, rows):
        for k, dx, device in ((0, 1, xp), (1, 3, xm)):
            state[name, k].wait_recv()
            add_into(dx, dy, pl.ds(start + k * quarter, quarter), via.at[slot, k])
            state["r" + name, k] = links.put(mine(dx, dy).at[rows], from_x.at[slot, k], device)

    def second():
        state["ya2"].wait_recv()
        add_into(2, 0, lower, ya.at[2])
        across("va", 2, (2, 0), 0)
        onward("vb1", 1, 1, half, upper)
        onward("vb0", 0, 0, half, upper)

    def third():
        for dx in (1, 3):
            state["ya%d" % dx].wait_recv()
            add_into(dx, 0, lower, ya.at[dx])
        onward("va", 2, 0, 0, lower)
        for k in range(2):
            state["rvb1", k].wait_recv()
        add_into(0, 1, upper, from_x.at[1, 0], from_x.at[1, 1])
        state["yb"] = links.put(mine(0, 1).at[upper], yb, yy)

    def fourth():
        state["ya0"].wait_recv()
        for k in range(2):
            state["rva", k].wait_recv()
        result[lower, :] = add(0, 0, lower, ya.at[0], from_x.at[2, 0], from_x.at[2, 1])[1]
        for k in range(2):
            state["rvb0", k].wait_recv()
        state["yb"].wait_recv()
        result[upper, :] = add(0, 0, upper, yb, from_x.at[0, 0], from_x.at[0, 1])[1]

    return first_a, first_b, second, third, fourth


def kernel(
    tile_hbm, target_ref, row_ref, wo_hbm, vw_hbm, query_hbm, key_hbm, value_hbm, position_ref, normed_hbm,
    gin_hbm, gq_ref, gk_ref, gow_ref, gvw_ref, vw_all,
    g_ref, query_ref, key_ref, value_ref, attended_ref, probs, weight, other, out_mine, core_out, core_value,
    ya_out, yb_out, via_out, x_out, ya_val, yb_val, via_val, x_val, gv_own, gv_all,
    hop, hop_target, hop_row, places, landed, landed_places, vw_own,
    relay_send, relay_recv, out_send, out_recv, value_send, value_recv, out_sum_send, out_sum_recv,
    value_sum_send, value_sum_recv, data_send, data_recv, place_send, place_recv, share_send, share_recv,
    core_send, core_recv, gv_send, gv_recv, gin_send, gin_recv, own_sem, tile_sem, local_sem, load_sem,
):
    at = Place()
    loads = [
        pltpu.make_async_copy(src, dst, load_sem.at[k])
        for k, (src, dst) in enumerate(((query_hbm, query_ref), (key_hbm, key_ref), (value_hbm, value_ref)))
    ]
    for load in loads:
        load.start()
    groups = 16
    tok, width = tile_hbm.shape
    chunks, _, cols = hop.shape
    across = (1 - at.s, at.w_y, at.n)
    barrier = greet(
        [across]
        + [at.wide((at.w + i) % groups) for i in range(1, groups)]
        + [(at.s, w, n) for w in (at.w, at.w_core) for n in (at.n_p, at.n_m, at.n_2)]
    )
    landed[:, :, SLOTS:, :] = jnp.zeros((chunks, groups, PAD - SLOTS, cols), landed.dtype)
    pl.semaphore_wait(barrier, 1 + 15 + 6)

    links = Links(relay_send, relay_recv)
    out_links = Links(out_send, out_recv)
    value_links = Links(value_send, value_recv)
    hop_index = [links.put(target_ref, hop_target, across), links.put(row_ref, hop_row, across)]
    hop_data = [links.put(tile_hbm.at[:, pl.ds(k * cols, cols)], hop.at[k], across) for k in range(chunks)]

    half_chunk = vw_hbm.shape[0] // 4

    def share(h, c):
        w, n = at.w - at.core + c, 2 * at.core + h
        src = vw_hbm.at[pl.ds((2 * h + c) * half_chunk, half_chunk)]
        dst = vw_own.at[pl.ds(pl.multiple_of(at.n * half_chunk, half_chunk), half_chunk)]
        mine = (at.core == c) & (at.n == n)
        remote = pltpu.make_async_remote_copy(
            src_ref=src, dst_ref=dst, send_sem=share_send.at[2 * h + c], recv_sem=share_recv.at[at.n],
            device_id=(at.s, w, n), device_id_type=MESH,
        )
        return mine, remote, lambda: pltpu.make_async_copy(src, dst, share_recv.at[at.n]).start()

    out_gather = gather_wide(at, out_links, wo_hbm, weight, local_sem.at[0])
    value_gather = gather_wide(at, value_links, vw_own, vw_all, local_sem.at[1])
    out_gather[0]()
    for h in range(2):
        for c in range(2):
            mine, remote, local = share(h, c)
            pl.when(mine)(local)
            pl.when(jnp.logical_not(mine))(remote.start)

    for copy in hop_index:
        copy.wait_recv()
    target = hop_target[...]
    group = lax.broadcasted_iota(jnp.int32, (groups, tok), 0)
    member = jnp.where(group == target, 1.0, 0.0).astype(jnp.float32)
    before = jnp.where(
        lax.broadcasted_iota(jnp.int32, (tok, tok), 0) < lax.broadcasted_iota(jnp.int32, (tok, tok), 1), 1.0, 0.0
    ).astype(jnp.bfloat16)
    earlier = jnp.dot(member.astype(jnp.bfloat16), before, preferred_element_type=jnp.float32)
    within = jnp.sum(earlier * member, axis=0, keepdims=True).astype(jnp.int32)
    slot = target * PAD + within

    def choose(r):
        return out_mine.at[4 + r // 2, :, pl.ds((r % 2) * tok, tok)]

    for r in range(4):
        wanted = lax.broadcasted_iota(jnp.int32, (256, tok), 0) + r * 256
        choose(r)[...] = jnp.where(wanted == slot, 1.0, 0.0).astype(jnp.bfloat16)

    lane = within + PAD * (at.w % 2)
    to_lane = jnp.where(
        lax.broadcasted_iota(jnp.int32, (128, tok), 0) == lane, 1.0, 0.0
    ).astype(jnp.bfloat16)
    place = hop_row[...] + 1
    high = (place // 32).astype(jnp.float32)
    low = (place % 32).astype(jnp.float32)
    high = lax.dot_general((member * high).astype(jnp.bfloat16), to_lane, NT, preferred_element_type=jnp.float32)
    low = lax.dot_general((member * low).astype(jnp.bfloat16), to_lane, NT, preferred_element_type=jnp.float32)
    lanes = (high * 32.0 + low).astype(jnp.int32)
    places[...] = jnp.broadcast_to(lanes[:, None, :], places.shape)

    def send_place(i):
        t = (at.w + i) % groups
        return pltpu.make_async_remote_copy(
            src_ref=places.at[t], dst_ref=landed_places.at[at.w],
            send_sem=place_send.at[t], recv_sem=place_recv.at[at.w],
            device_id=at.wide(t), device_id_type=MESH,
        )

    def from_packed(k, t):
        rows = pl.ds(pl.multiple_of((t % 4) * PAD, PAD), SLOTS)
        return out_mine.at[t // 4, rows, pl.ds(k * cols, cols)], landed.at[k, at.w, pl.ds(0, SLOTS)]

    def send_rows(k, i):
        t = (at.w + i) % groups
        src, dst = from_packed(k, t)
        return pltpu.make_async_remote_copy(
            src_ref=src, dst_ref=dst, send_sem=data_send.at[k, t], recv_sem=data_recv.at[k, at.w],
            device_id=at.wide(t), device_id_type=MESH,
        )

    pltpu.make_async_copy(places.at[at.w], landed_places.at[at.w], place_recv.at[at.w]).start()

    @pl.loop(1, groups)
    def _(i):
        send_place(i).start()

    def pack(k):
        hop_data[k].wait_recv()
        for r in range(4):
            rows = jnp.dot(choose(r)[...], hop[k], preferred_element_type=jnp.float32)
            out_mine[r, :, pl.ds(k * cols, cols)] = rows.astype(jnp.bfloat16)
        src, dst = from_packed(k, at.w)
        pltpu.make_async_copy(src, dst, data_recv.at[k, at.w]).start()

        @pl.loop(1, groups)
        def _(i):
            send_rows(k, i).start()

    part = tok // 2
    z_p, z_m, on_p, on_m = [], [], [], []

    def unpack(k):
        @pl.loop(0, groups)
        def _(i):
            piece = landed.at[k, i, pl.ds(0, SLOTS)]
            pltpu.make_async_copy(piece, piece, data_recv.at[k, i]).wait()

        rows = landed[k].reshape(groups * PAD, cols)
        for r in range(2):
            placed = jnp.dot(out_mine[6 + r], rows, preferred_element_type=jnp.float32)
            g_ref[at.n, pl.ds(r * part, part), pl.ds(k * cols, cols)] = placed.astype(jnp.bfloat16)
        ref = g_ref.at[at.n, :, pl.ds(k * cols, cols)]
        z_p.append(links.put(ref, ref, at.narrow(at.n_p)))
        z_m.append(links.put(ref, ref, at.narrow(at.n_m)))

    def forward(k):
        z_p[k].wait_recv()
        ref = g_ref.at[at.n_m, pl.ds(0, part), pl.ds(k * cols, cols)]
        on_p.append(links.put(ref, ref, at.narrow(at.n_p)))
        z_m[k].wait_recv()
        ref = g_ref.at[at.n_p, pl.ds(part, part), pl.ds(k * cols, cols)]
        on_m.append(links.put(ref, ref, at.narrow(at.n_m)))

    key_at = lax.broadcasted_iota(jnp.int32, (tok, tok), 0)
    query_at = lax.broadcasted_iota(jnp.int32, (tok, tok), 1)
    earliest = lax.broadcasted_iota(jnp.int32, (1, tok), 1) - position_ref[...]

    def heads(first, last):
        @pl.loop(first, last)
        def _(head):
            allowed = (key_at <= query_at) & (key_at >= earliest)
            attention_forward(head, query_ref, key_ref, value_ref, allowed, probs, attended_ref)

    def wait_places():
        @pl.loop(0, groups)
        def _(i):
            piece = landed_places.at[i]
            pltpu.make_async_copy(piece, piece, place_recv.at[i]).wait()

        arrived = landed_places[...].reshape(groups // 2, 2, 8, 128)
        arrived = (arrived[:, 0] + arrived[:, 1])[:, 0, :]
        for r in range(2):
            token = lax.broadcasted_iota(jnp.int32, (part, 128), 0) + (1 + r * part)
            for k in range(groups // 2):
                here = jnp.where(token == arrived[k : k + 1, :], 1.0, 0.0)
                out_mine[6 + r, :, pl.ds(k * 128, 128)] = here.astype(jnp.bfloat16)

    pack(0)
    for load in loads:
        load.wait()
    heads(0, 2)
    wait_places()
    pack(1)
    out_gather[1]()
    out_gather[2]()
    unpack(0)
    for b in range(4):
        piece = vw_own.at[pl.ds(b * half_chunk, half_chunk)]
        pltpu.make_async_copy(piece, piece, share_recv.at[b]).wait()
    value_gather[0]()
    pack(2)
    unpack(1)
    heads(2, 4)
    pack(3)
    out_gather[3]()
    unpack(2)
    forward(0)
    unpack(3)
    heads(4, 6)
    forward(1)
    value_gather[1]()
    value_gather[2]()
    heads(6, 8)
    out_gather[4]()
    forward(2)

    @pl.loop(1, groups)
    def _(i):
        send_place(i).wait_send()
        for k in range(chunks):
            send_rows(k, i).wait_send()

    out_scatter = Links(out_sum_send, out_sum_recv)
    value_scatter = Links(value_sum_send, value_sum_recv)

    def chip(dx, dy):
        y = at.y if dy == 0 else 1 - at.y
        return ((at.x + dx) % 4) * 2 + y

    def far_first(i):
        return (at.x + 2 + i // 2) % 4, (at.y + 1 + i) % 2

    def as_arriving(i):
        k = i // 2
        return (at.n + k + k // 2 - 2 * (k // 3)) % 4, i % 2

    def terms(which, chip_of, left, right, to_core, mine, landing):
        def send(i):
            x, y = chip_of(i)
            return pltpu.make_async_remote_copy(
                src_ref=to_core(x, y), dst_ref=landing.at[x * 2 + y],
                send_sem=core_send.at[which, i], recv_sem=core_recv.at[which, i],
                device_id=at.wide(at.w_core), device_id_type=MESH,
            )

        def theirs(first, last):
            @pl.loop(first, last)
            def _(i):
                x, y = chip_of(i)
                term = lax.dot_general(left(x, y, 1 - at.core), right[...], TN, preferred_element_type=jnp.float32)
                to_core(x, y)[...] = term.astype(jnp.bfloat16)
                send(i).start()

        def ours(first, last):
            @pl.loop(first, last)
            def _(i):
                x, y = chip_of(i)
                term = lax.dot_general(left(x, y, at.core), right[...], TN, preferred_element_type=jnp.float32)
                send(i).wait_recv()
                term = term + landing[x * 2 + y].astype(jnp.float32)
                mine(x * 2 + y)[...] = term.astype(jnp.bfloat16)

        def drain():
            @pl.loop(0, 8)
            def _(i):
                send(i).wait_send()

        return theirs, ours, drain

    def g_columns(x, y, core):
        return g_ref[x, :, pl.ds(pl.multiple_of(y * 512 + core * 256, 256), 256)]

    def normed_columns(x, y, core):
        return other[:, pl.ds(pl.multiple_of(x * 1024 + y * 512 + core * 256, 256), 256)]

    def in_other(x, y):
        return other.at[pl.ds(pl.multiple_of(y * 256, 256), 256), pl.ds(pl.multiple_of(x * 1024, 1024), 1024)]

    theirs, ours, drain_core = terms(0, as_arriving, g_columns, attended_ref, in_other, lambda j: out_mine.at[j], core_out)
    out_steps = scatter_wide(
        at, out_scatter, lambda dx, dy: out_mine.at[chip(dx, dy)], (ya_out, yb_out), via_out, x_out, gow_ref
    )
    theirs(0, 2)
    forward(3)
    theirs(2, 6)
    ours(0, 6)
    value_gather[3]()
    for k in range(chunks):
        on_p[k].wait_recv()
        on_m[k].wait_recv()
    theirs(6, 8)
    ours(6, 8)
    out_steps[0]()
    out_steps[1]()
    drain_core()
    load_normed = pltpu.make_async_copy(normed_hbm, other, local_sem.at[2])
    load_normed.start()
    out_gather[5]()

    scale = HEAD_DIM**-0.5

    def gv_copies(pair):
        def copy(k, src, device):
            return pltpu.make_async_remote_copy(
                src_ref=src, dst_ref=src, send_sem=gv_send.at[k, pair], recv_sem=gv_recv.at[k, pair],
                device_id=at.narrow(device), device_id_type=MESH,
            )

        mine = gv_all.at[at.n, pair]
        on_p = gv_all.at[at.n_m, pair, pl.ds(0, part)]
        on_m = gv_all.at[at.n_p, pair, pl.ds(part, part)]
        return copy(0, mine, at.n_p), copy(1, mine, at.n_m), copy(2, on_p, at.n_p), copy(3, on_m, at.n_m)

    def forward_gv(pair):
        to_p, to_m, on_p, on_m = gv_copies(pair)
        to_p.wait_recv()
        on_p.start()
        to_m.wait_recv()
        on_m.start()

    def attend(pair):
        lanes = pl.ds(pair * 256, 256)
        total = jnp.zeros((tok, 256), jnp.float32)
        for b in range(4):
            block = weight[4 * b : 4 * b + 4, :, lanes].reshape(width, 256)
            total = total + jnp.dot(g_ref[b], block, preferred_element_type=jnp.float32)
        both = total.astype(jnp.bfloat16)
        for h in range(2):
            cols = pl.ds(pair * 256 + h * HEAD_DIM, HEAD_DIM)
            gout = both[:, h * HEAD_DIM : (h + 1) * HEAD_DIM]
            prob = probs[2 * pair + h]
            dprob = lax.dot_general(value_ref[:, cols], gout, NT, preferred_element_type=jnp.float32)
            wide_prob = prob.astype(jnp.float32)
            delta = jnp.sum(wide_prob * dprob, axis=0, keepdims=True)
            dscore = (wide_prob * (dprob - delta)).astype(jnp.bfloat16)
            gv = jnp.dot(prob, gout, preferred_element_type=jnp.float32).astype(jnp.bfloat16)
            gv_own[:, cols] = gv
            gv_all[at.n, pair, :, pl.ds(h * HEAD_DIM, HEAD_DIM)] = gv
            gk = jnp.dot(dscore, query_ref[:, cols], preferred_element_type=jnp.float32) * scale
            gk_ref[:, cols] = gk.astype(jnp.bfloat16)
            gq = lax.dot_general(dscore, key_ref[:, cols], TN, preferred_element_type=jnp.float32) * scale
            gq_ref[:, cols] = gq.astype(jnp.bfloat16)
        to_p, to_m, _, _ = gv_copies(pair)
        to_p.start()
        to_m.start()
        if pair > 0:
            forward_gv(pair - 1)

    attend(0)
    attend(1)
    value_gather[4]()
    attend(2)
    out_steps[2]()
    attend(3)
    out_steps[3]()
    out_links.drain()

    def load_tile(tile):
        return pltpu.make_async_copy(vw_all.at[pl.ds(4 * tile, 4)], core_out.at[pl.ds(4 * (tile % 2), 4)], tile_sem.at[tile % 2])

    load_normed.wait()
    theirs, ours, drain_value = terms(
        1, far_first, normed_columns, gv_own, lambda x, y: weight.at[x * 2 + y], lambda j: weight.at[8 + j], core_value
    )
    value_steps = scatter_wide(
        at, value_scatter, lambda dx, dy: weight.at[8 + chip(dx, dy)], (ya_val, yb_val), via_val, x_val, gvw_ref
    )
    theirs(0, 8)
    forward_gv(3)
    ours(0, 2)
    value_steps[0]()
    ours(2, 8)
    value_steps[1]()
    value_gather[5]()
    load_tile(0).start()
    load_tile(1).start()
    for pair in range(4):
        _, _, on_p, on_m = gv_copies(pair)
        on_p.wait_recv()
        on_m.wait_recv()

    def gin_copies(tile, y):
        def copy(k, src, dst, device):
            return pltpu.make_async_remote_copy(
                src_ref=src, dst_ref=dst, send_sem=gin_send.at[k, 2 * tile + y], recv_sem=gin_recv.at[k, 2 * tile + y],
                device_id=at.narrow(device), device_id_type=MESH,
            )

        def chunk(n, start, size):
            cols = pl.ds(pl.multiple_of(tile * 1024 + y * 512 + n * 128, 128), 128)
            return gin_hbm.at[pl.ds(start, size), cols]

        src, dst = hop.at[tile, :, pl.ds(y * 128, 128)], chunk(at.n, 0, tok)
        on_p, on_m = chunk(at.n_m, 0, part), chunk(at.n_p, part, part)
        own = pltpu.make_async_copy(src, dst, own_sem.at[2 * tile + y])
        return copy(0, src, dst, at.n_p), copy(1, src, dst, at.n_m), copy(2, on_p, on_p, at.n_p), copy(3, on_m, on_m, at.n_m), own

    def forward_gin(tile):
        for y in range(2):
            to_p, to_m, on_p, on_m, _ = gin_copies(tile, y)
            to_p.wait_recv()
            on_p.start()
            to_m.wait_recv()
            on_m.start()

    for tile in range(4):
        load_tile(tile).wait()
        chunk = pl.multiple_of(at.n * 128, 128)
        low = g_ref[tile, :, pl.ds(chunk, 128)]
        high = g_ref[tile, :, pl.ds(pl.multiple_of(chunk + 512, 128), 128)]
        total = jnp.concatenate([low, high], axis=1).astype(jnp.float32)
        for z in range(4):
            for pair in range(4):
                block = core_out[
                    4 * (tile % 2) : 4 * (tile % 2) + 4, z * 64 : (z + 1) * 64, pair * 256 : (pair + 1) * 256
                ].reshape(256, 256)
                total = total + lax.dot_general(gv_all[z, pair], block, NT, preferred_element_type=jnp.float32)
        hop[tile] = total.astype(jnp.bfloat16)
        for y in range(2):
            to_p, to_m, _, _, own = gin_copies(tile, y)
            to_p.start()
            to_m.start()
            own.start()
        if tile < 2:
            load_tile(tile + 2).start()

    out_steps[4]()
    forward_gin(0)
    value_steps[2]()
    forward_gin(1)
    forward_gin(2)
    value_steps[3]()
    forward_gin(3)
    value_steps[4]()
    drain_value()
    for tile in range(4):
        for y in range(2):
            to_p, to_m, on_p, on_m, own = gin_copies(tile, y)
            on_p.wait_recv()
            on_m.wait_recv()
            own.wait()
            for copy in (to_p, to_m, on_p, on_m):
                copy.wait_send()
        for copy in gv_copies(tile):
            copy.wait_send()
    for h in range(2):
        for c in range(2):
            mine, remote, local = share(h, c)
            pl.when(jnp.logical_not(mine))(remote.wait_send)

    for used in (links, value_links, out_scatter, value_scatter):
        used.drain()


def backward(tile, target, row, wo, vw, query, key, value, position, normed):
    tok, width = tile.shape
    rows = wo.shape[0]
    half = rows // 2
    chunks = 4
    bf16, f32, i32 = jnp.bfloat16, jnp.float32, jnp.int32
    dma = pltpu.SemaphoreType.DMA
    vmem = pl.BlockSpec(memory_space=pltpu.VMEM)
    hbm = pl.BlockSpec(memory_space=pl.ANY)

    def buffer(*shape):
        return pltpu.VMEM(shape, bf16)

    landing = [
        buffer(4, half, width),
        buffer(half, width),
        buffer(3, 2, half // 2, width),
        buffer(3, 2, half, width),
    ]
    return pl.pallas_call(
        kernel,
        out_shape=(
            jax.ShapeDtypeStruct((tok, 4 * width), bf16),
            jax.ShapeDtypeStruct((tok, width), bf16),
            jax.ShapeDtypeStruct((tok, width), bf16),
            jax.ShapeDtypeStruct((rows, width), f32),
            jax.ShapeDtypeStruct((rows, width), f32),
            jax.ShapeDtypeStruct((16, rows, width), bf16),
        ),
        in_specs=[hbm, vmem, vmem, hbm, hbm, hbm, hbm, hbm, vmem, hbm],
        out_specs=(hbm, vmem, vmem, vmem, vmem, hbm),
        scratch_shapes=[
            buffer(4, tok, width),
            *[buffer(tok, width)] * 4,
            buffer(width // HEAD_DIM, tok, tok),
            buffer(16, rows, width),
            buffer(tok, 4 * width),
            *[buffer(8, rows, width)] * 3,
            *landing,
            *landing,
            buffer(tok, width),
            buffer(4, 4, tok, 256),
            buffer(chunks, tok, width // chunks),
            pltpu.VMEM(target.shape, i32),
            pltpu.VMEM(row.shape, i32),
            pltpu.VMEM((16, 8, 128), i32),
            buffer(chunks, 16, PAD, width // chunks),
            pltpu.VMEM((16, 8, 128), i32),
            buffer(rows, width),
            *[dma((22,))] * 2,
            *[dma((20,))] * 4,
            *[dma((17,))] * 4,
            *[dma((chunks, 16))] * 2,
            *[dma((16,))] * 2,
            *[dma((4,))] * 2,
            *[dma((2, 8))] * 2,
            *[dma((4, 4))] * 2,
            *[dma((4, 8))] * 2,
            dma((8,)), dma((2,)), dma((3,)), dma((3,)),
        ],
        compiler_params=pltpu.CompilerParams(
            collective_id=0, has_side_effects=True, vmem_limit_bytes=63 * 1024 * 1024
        ),
        name="relay_backward_and_sum",
    )(tile, target, row, wo, vw, query, key, value, position, normed)


def shards(boundary_grad, tile_target, tile_row, normed_input, query, keys, values, positions, out_weight, value_weight):
    outputs = backward(
        boundary_grad[0], tile_target, tile_row, out_weight[0], value_weight[0], query[0], keys[0], values[0], positions,
        normed_input[0],
    )
    return tuple(output[None] for output in outputs[:5])


def solution(mesh):
    split = P("section", "wide", "narrow")
    rows = P("section", "wide")
    in_specs = (split, rows, rows, P("section", "wide", None), split, split, split, rows, split, split)
    out_specs = (P("section", "wide", None), split, split, split, split)
    return jax.shard_map(shards, mesh=mesh, in_specs=in_specs, out_specs=out_specs, check_vma=False)
```

```python
import functools

import jax
import jax.numpy as jnp
from jax import lax
from jax.experimental import pallas as pl
from jax.experimental.pallas import tpu as pltpu
from jax.sharding import PartitionSpec as P

HEAD_DIM = 128
MESH = pl.DeviceIdType.MESH
NT = (((1,), (1,)), ((), ()))
TN = (((0,), (0,)), ((), ()))
SLOTS = 48
PAD = 64


class Place:
    def __init__(self):
        self.s = lax.axis_index("section")
        self.w = lax.axis_index("wide")
        self.n = lax.axis_index("narrow")
        self.core = self.w % 2
        self.y = (self.w // 2) % 2
        self.x = self.w // 4
        self.w_xp = (self.w + 4) % 16
        self.w_xm = (self.w + 12) % 16
        self.w_x2 = (self.w + 8) % 16
        self.w_y = self.w + 2 - 4 * self.y
        self.w_core = self.w + 1 - 2 * self.core
        self.y_xp = (self.w_y + 4) % 16
        self.y_xm = (self.w_y + 12) % 16
        self.y_x2 = (self.w_y + 8) % 16
        self.n_p = (self.n + 1) % 4
        self.n_m = (self.n + 3) % 4
        self.n_2 = (self.n + 2) % 4

    def wide(self, w):
        return (self.s, w, self.n)

    def narrow(self, n):
        return (self.s, self.w, n)


class Links:
    def __init__(self, send_sem, recv_sem):
        self.send_sem, self.recv_sem, self.count, self.sent = send_sem, recv_sem, 0, []

    def put(self, src, dst, device):
        copy = pltpu.make_async_remote_copy(
            src_ref=src,
            dst_ref=dst,
            send_sem=self.send_sem.at[self.count],
            recv_sem=self.recv_sem.at[self.count],
            device_id=device,
            device_id_type=MESH,
        )
        copy.start()
        self.count += 1
        self.sent.append(copy)
        return copy

    def drain(self):
        for copy in self.sent:
            copy.wait_send()


def greet(devices):
    barrier = pltpu.get_barrier_semaphore()
    for device in devices:
        pl.semaphore_signal(barrier, inc=1, device_id=device, device_id_type=MESH)
    return barrier


def split_rows(rows):
    low = rows * 7 // 16
    return low, low + rows // 4


def gather_wide(at, links, own, full, local_sem):
    rows = own.shape[0]
    low, middle = split_rows(rows)
    lower, upper = pl.ds(0, low), pl.ds(low, rows - low)
    third, fourth = pl.ds(low, middle - low), pl.ds(middle, rows - middle)
    one, two = pl.ds(0, rows // 2), pl.ds(rows // 2, rows // 2)
    xp, xm, yy, cc = (at.wide(w) for w in (at.w_xp, at.w_xm, at.w_y, at.w_core))

    def send(w, device, rows=None):
        ref = full.at[w] if rows is None else full.at[w, rows]
        return links.put(ref, ref, device)

    state = {}

    def first():
        state["own"] = pltpu.make_async_copy(own, full.at[at.w], local_sem)
        state["own"].start()
        state["y"] = links.put(own, full.at[at.w], yy)
        state["xp"] = links.put(own, full.at[at.w], xp)
        state["xm"] = links.put(own, full.at[at.w], xm)
        state["core"] = links.put(own, full.at[at.w], cc)

    def second_y():
        state["y"].wait_recv()
        state["b_p"] = send(at.w_y, xp, upper)
        state["b_m"] = send(at.w_y, xm, upper)
        state["c_y"] = send(at.w_y, cc)

    def second_x():
        state["xp"].wait_recv()
        state["f_p"] = send(at.w_xm, xp, one)
        state["g_m"] = send(at.w_xm, yy, lower)
        state["c_m"] = send(at.w_xm, cc)
        state["xm"].wait_recv()
        state["f_m"] = send(at.w_xp, xm, two)
        state["g_p"] = send(at.w_xp, yy, lower)
        state["c_p"] = send(at.w_xp, cc)

    def third_step():
        state["b_p"].wait_recv()
        state["h_p"] = send(at.y_xm, xp, third)
        state["b_m"].wait_recv()
        state["h_m"] = send(at.y_xp, xm, fourth)
        state["f_p"].wait_recv()
        state["g_2"] = send(at.w_x2, yy, lower)
        state["f_m"].wait_recv()
        state["c_2"] = send(at.w_x2, cc)

    def fourth_step():
        state["g_m"].wait_recv()
        state["e_m"] = send(at.y_xm, cc)
        state["g_p"].wait_recv()
        state["e_p"] = send(at.y_xp, cc)
        state["h_p"].wait_recv()
        state["h_m"].wait_recv()
        state["g_2"].wait_recv()
        state["e_2"] = send(at.y_x2, cc)

    def last():
        state["own"].wait()
        for name in ("core", "c_y", "c_m", "c_p", "c_2", "e_m", "e_p", "e_2"):
            state[name].wait_recv()

    return first, second_y, second_x, third_step, fourth_step, last


def attention_forward(head, query_ref, key_ref, value_ref, allowed, probs_ref, attended_ref):
    lanes = pl.ds(pl.multiple_of(head * HEAD_DIM, HEAD_DIM), HEAD_DIM)
    scores = lax.dot_general(key_ref[:, lanes], query_ref[:, lanes], NT, preferred_element_type=jnp.float32)
    scores = jnp.where(allowed, scores * HEAD_DIM**-0.5, -1e30)
    weights = jnp.exp(scores - jnp.max(scores, axis=0, keepdims=True))
    probs = (weights / jnp.sum(weights, axis=0, keepdims=True)).astype(jnp.bfloat16)
    probs_ref[head] = probs
    attended = lax.dot_general(probs, value_ref[:, lanes], TN, preferred_element_type=jnp.float32)
    attended_ref[:, lanes] = attended.astype(jnp.bfloat16)


def scatter_wide(at, links, mine, from_y, via, from_x, result):
    rows = result.shape[0]
    low, middle = split_rows(rows)
    lower, upper = pl.ds(0, low), pl.ds(low, rows - low)
    low_parts = pl.ds(0, rows // 4), pl.ds(rows // 4, low - rows // 4)
    high_parts = pl.ds(low, middle - low), pl.ds(middle, rows - middle)
    xp, xm, yy = (at.wide(w) for w in (at.w_xp, at.w_xm, at.w_y))
    ya, yb = from_y
    state = {}

    def add(dx, dy, rows, *others):
        ref = mine(dx, dy).at[rows]
        total = ref[...].astype(jnp.float32)
        for other in others:
            total = total + other[...].astype(jnp.float32)
        return ref, total

    def add_into(dx, dy, rows, *others):
        ref, total = add(dx, dy, rows, *others)
        ref[...] = total.astype(jnp.bfloat16)

    def across(name, slot, dx_dy, parts):
        for k, device in ((0, xp), (1, xm)):
            landing = via.at[slot, k, pl.ds(0, parts[k].size)]
            state[name, k] = links.put(mine(*dx_dy).at[parts[k]], landing, device)

    def first_a():
        state["ya2"] = links.put(mine(2, 1).at[lower], ya.at[2], yy)
        across("vb1", 1, (2, 1), high_parts)
        across("vb0", 0, (2, 0), high_parts)

    def first_b():
        for dx in (1, 3, 0):
            state["ya%d" % dx] = links.put(mine(dx, 1).at[lower], ya.at[dx], yy)

    def onward(name, slot, dy, parts, rows):
        for k, dx, device in ((0, 1, xp), (1, 3, xm)):
            state[name, k].wait_recv()
            add_into(dx, dy, parts[k], via.at[slot, k, pl.ds(0, parts[k].size)])
            landing = from_x.at[slot, k, pl.ds(0, rows.size)]
            state["r" + name, k] = links.put(mine(dx, dy).at[rows], landing, device)

    def second():
        state["ya2"].wait_recv()
        add_into(2, 0, lower, ya.at[2])
        across("va", 2, (2, 0), low_parts)
        onward("vb1", 1, 1, high_parts, upper)
        onward("vb0", 0, 0, high_parts, upper)

    def upper_from_x(slot):
        return [from_x.at[slot, k] for k in range(2)]

    def third():
        for dx in (1, 3):
            state["ya%d" % dx].wait_recv()
            add_into(dx, 0, lower, ya.at[dx])
        onward("va", 2, 0, low_parts, lower)
        for k in range(2):
            state["rvb1", k].wait_recv()
        add_into(0, 1, upper, *upper_from_x(1))
        state["yb"] = links.put(mine(0, 1).at[upper], yb, yy)

    def fourth():
        state["ya0"].wait_recv()
        for k in range(2):
            state["rva", k].wait_recv()
        lower_from_x = [from_x.at[2, k, pl.ds(0, low)] for k in range(2)]
        result[lower, :] = add(0, 0, lower, ya.at[0], *lower_from_x)[1]
        for k in range(2):
            state["rvb0", k].wait_recv()
        state["yb"].wait_recv()
        result[upper, :] = add(0, 0, upper, yb, *upper_from_x(0))[1]

    return first_a, first_b, second, third, fourth


def kernel(
    tile_hbm, target_ref, row_ref, wo_hbm, vw_hbm, query_hbm, key_hbm, value_hbm, position_ref, normed_hbm,
    gin_hbm, gq_hbm, gk_hbm, gow_hbm, gvw_hbm, vw_all,
    gq_ref, gk_ref, gow_ref, gvw_ref,
    g_ref, query_ref, key_ref, value_ref, attended_ref, probs, weight, other, out_mine, core_out, core_value,
    ya_out, yb_out, via_out, x_out, ya_val, yb_val, via_val, x_val, gv_own, gv_all,
    hop, hop_slot, hop_places, slots, places, landed, landed_places, vw_own,
    relay_send, relay_recv, out_send, out_recv, value_send, value_recv, out_sum_send, out_sum_recv,
    value_sum_send, value_sum_recv, data_send, data_recv, place_send, place_recv, share_send, share_recv,
    core_send, core_recv, gv_send, gv_recv, gin_send, gin_recv, own_sem, tile_sem, local_sem, load_sem, store_sem,
):
    at = Place()
    loads = [
        pltpu.make_async_copy(src, dst, load_sem.at[k])
        for k, (src, dst) in enumerate(((query_hbm, query_ref), (key_hbm, key_ref), (value_hbm, value_ref)))
    ]
    for load in loads:
        load.start()
    groups = 16
    tok, width = tile_hbm.shape
    chunks, _, cols = hop.shape
    across = (1 - at.s, at.w_y, at.n)
    barrier = greet(
        [across]
        + [at.wide((at.w + i) % groups) for i in range(1, groups)]
        + [(at.s, w, n) for w in (at.w, at.w_core) for n in (at.n_p, at.n_m, at.n_2)]
    )
    target = target_ref[...]
    group = lax.broadcasted_iota(jnp.int32, (groups, tok), 0)
    member = jnp.where(group == target, 1.0, 0.0).astype(jnp.float32)
    before = jnp.where(
        lax.broadcasted_iota(jnp.int32, (tok, tok), 0) < lax.broadcasted_iota(jnp.int32, (tok, tok), 1), 1.0, 0.0
    ).astype(jnp.bfloat16)
    earlier = jnp.dot(member.astype(jnp.bfloat16), before, preferred_element_type=jnp.float32)
    within = jnp.sum(earlier * member, axis=0, keepdims=True).astype(jnp.int32)
    slots[...] = jnp.broadcast_to(target * PAD + within, slots.shape)
    lane = within + PAD * (at.w % 2)
    to_lane = jnp.where(
        lax.broadcasted_iota(jnp.int32, (128, tok), 0) == lane, 1.0, 0.0
    ).astype(jnp.bfloat16)
    place = row_ref[...] + 1
    high = (place // 32).astype(jnp.float32)
    low = (place % 32).astype(jnp.float32)
    high = lax.dot_general((member * high).astype(jnp.bfloat16), to_lane, NT, preferred_element_type=jnp.float32)
    low = lax.dot_general((member * low).astype(jnp.bfloat16), to_lane, NT, preferred_element_type=jnp.float32)
    lanes = (high * 32.0 + low).astype(jnp.int32)
    places[...] = jnp.broadcast_to(lanes[:, None, :], places.shape)
    landed[:, :, SLOTS:, :] = jnp.zeros((chunks, groups, PAD - SLOTS, cols), landed.dtype)
    pl.semaphore_wait(barrier, 1 + 15 + 6)

    links = Links(relay_send, relay_recv)
    out_links = Links(out_send, out_recv)
    value_links = Links(value_send, value_recv)
    hop_index = [links.put(slots, hop_slot, across), links.put(places, hop_places, across)]
    hop_data = [links.put(tile_hbm.at[:, pl.ds(k * cols, cols)], hop.at[k], across) for k in range(chunks)]

    half_chunk = vw_hbm.shape[0] // 4

    def share(h, c):
        w, n = at.w - at.core + c, 2 * at.core + h
        src = vw_hbm.at[pl.ds((2 * h + c) * half_chunk, half_chunk)]
        dst = vw_own.at[pl.ds(pl.multiple_of(at.n * half_chunk, half_chunk), half_chunk)]
        mine = (at.core == c) & (at.n == n)
        remote = pltpu.make_async_remote_copy(
            src_ref=src, dst_ref=dst, send_sem=share_send.at[2 * h + c], recv_sem=share_recv.at[at.n],
            device_id=(at.s, w, n), device_id_type=MESH,
        )
        return mine, remote, lambda: pltpu.make_async_copy(src, dst, share_recv.at[at.n]).start()

    out_gather = gather_wide(at, out_links, wo_hbm, weight, local_sem.at[0])
    value_gather = gather_wide(at, value_links, vw_own, vw_all, local_sem.at[1])
    out_gather[0]()
    for h in range(2):
        for c in range(2):
            mine, remote, local = share(h, c)
            pl.when(mine)(local)
            pl.when(jnp.logical_not(mine))(remote.start)

    hop_index[0].wait_recv()
    slot = hop_slot[0:1, :]

    def choose(r):
        return out_mine.at[4 + r // 2, :, pl.ds((r % 2) * tok, tok)]

    for r in range(4):
        wanted = lax.broadcasted_iota(jnp.int32, (256, tok), 0) + r * 256
        choose(r)[...] = jnp.where(wanted == slot, 1.0, 0.0).astype(jnp.bfloat16)

    hop_index[1].wait_recv()

    def send_place(i):
        t = (at.w + i) % groups
        return pltpu.make_async_remote_copy(
            src_ref=hop_places.at[t], dst_ref=landed_places.at[at.w],
            send_sem=place_send.at[t], recv_sem=place_recv.at[at.w],
            device_id=at.wide(t), device_id_type=MESH,
        )

    def from_packed(k, t):
        rows = pl.ds(pl.multiple_of((t % 4) * PAD, PAD), SLOTS)
        return out_mine.at[t // 4, rows, pl.ds(k * cols, cols)], landed.at[k, at.w, pl.ds(0, SLOTS)]

    def send_rows(k, i):
        t = (at.w + i) % groups
        src, dst = from_packed(k, t)
        return pltpu.make_async_remote_copy(
            src_ref=src, dst_ref=dst, send_sem=data_send.at[k, t], recv_sem=data_recv.at[k, at.w],
            device_id=at.wide(t), device_id_type=MESH,
        )

    pltpu.make_async_copy(hop_places.at[at.w], landed_places.at[at.w], place_recv.at[at.w]).start()

    @pl.loop(1, groups)
    def _(i):
        send_place(i).start()

    def pack(k):
        hop_data[k].wait_recv()
        for r in range(4):
            rows = jnp.dot(choose(r)[...], hop[k], preferred_element_type=jnp.float32)
            out_mine[r, :, pl.ds(k * cols, cols)] = rows.astype(jnp.bfloat16)
        src, dst = from_packed(k, at.w)
        pltpu.make_async_copy(src, dst, data_recv.at[k, at.w]).start()

        @pl.loop(1, groups)
        def _(i):
            send_rows(k, i).start()

    part = tok // 2
    z_p, z_m, on_p, on_m = [], [], [], []

    def unpack(k):
        @pl.loop(0, groups)
        def _(i):
            piece = landed.at[k, i, pl.ds(0, SLOTS)]
            pltpu.make_async_copy(piece, piece, data_recv.at[k, i]).wait()

        rows = landed[k].reshape(groups * PAD, cols)
        for r in range(2):
            placed = jnp.dot(out_mine[6 + r], rows, preferred_element_type=jnp.float32)
            g_ref[at.n, pl.ds(r * part, part), pl.ds(k * cols, cols)] = placed.astype(jnp.bfloat16)
        ref = g_ref.at[at.n, :, pl.ds(k * cols, cols)]
        z_p.append(links.put(ref, ref, at.narrow(at.n_p)))
        z_m.append(links.put(ref, ref, at.narrow(at.n_m)))

    def forward(k):
        z_p[k].wait_recv()
        ref = g_ref.at[at.n_m, pl.ds(0, part), pl.ds(k * cols, cols)]
        on_p.append(links.put(ref, ref, at.narrow(at.n_p)))
        z_m[k].wait_recv()
        ref = g_ref.at[at.n_p, pl.ds(part, part), pl.ds(k * cols, cols)]
        on_m.append(links.put(ref, ref, at.narrow(at.n_m)))

    key_at = lax.broadcasted_iota(jnp.int32, (tok, tok), 0)
    query_at = lax.broadcasted_iota(jnp.int32, (tok, tok), 1)
    earliest = lax.broadcasted_iota(jnp.int32, (1, tok), 1) - position_ref[...]

    def heads(first, last):
        @pl.loop(first, last)
        def _(head):
            allowed = (key_at <= query_at) & (key_at >= earliest)
            attention_forward(head, query_ref, key_ref, value_ref, allowed, probs, attended_ref)

    def wait_places():
        @pl.loop(0, groups)
        def _(i):
            piece = landed_places.at[i]
            pltpu.make_async_copy(piece, piece, place_recv.at[i]).wait()

        arrived = landed_places[...].reshape(groups // 2, 2, 8, 128)
        arrived = (arrived[:, 0] + arrived[:, 1])[:, 0, :]
        for r in range(2):
            token = lax.broadcasted_iota(jnp.int32, (part, 128), 0) + (1 + r * part)
            for k in range(groups // 2):
                here = jnp.where(token == arrived[k : k + 1, :], 1.0, 0.0)
                out_mine[6 + r, :, pl.ds(k * 128, 128)] = here.astype(jnp.bfloat16)

    def wait_loads():
        for load in loads:
            load.wait()

    def wait_share():
        for b in range(4):
            piece = vw_own.at[pl.ds(b * half_chunk, half_chunk)]
            pltpu.make_async_copy(piece, piece, share_recv.at[b]).wait()

    def drain_rows():
        @pl.loop(1, groups)
        def _(i):
            send_place(i).wait_send()
            for k in range(chunks):
                send_rows(k, i).wait_send()

    def wait_gathered():
        for k in range(chunks):
            on_p[k].wait_recv()
            on_m[k].wait_recv()

    out_scatter = Links(out_sum_send, out_sum_recv)
    value_scatter = Links(value_sum_send, value_sum_recv)

    def chip(dx, dy):
        y = at.y if dy == 0 else 1 - at.y
        return ((at.x + dx) % 4) * 2 + y

    def far_first(i):
        return (at.x + 2 + i // 2) % 4, (at.y + 1 + i) % 2

    def as_arriving(i):
        k = i // 2
        return (at.n + k + k // 2 - 2 * (k // 3)) % 4, i % 2

    def terms(which, chip_of, left, right, to_core, mine, landing):
        def send(i):
            x, y = chip_of(i)
            return pltpu.make_async_remote_copy(
                src_ref=to_core(x, y), dst_ref=landing.at[x * 2 + y],
                send_sem=core_send.at[which, i], recv_sem=core_recv.at[which, i],
                device_id=at.wide(at.w_core), device_id_type=MESH,
            )

        def theirs(first, last):
            @pl.loop(first, last)
            def _(i):
                x, y = chip_of(i)
                term = lax.dot_general(left(x, y, 1 - at.core), right[...], TN, preferred_element_type=jnp.float32)
                to_core(x, y)[...] = term.astype(jnp.bfloat16)
                send(i).start()

        def ours(first, last):
            @pl.loop(first, last)
            def _(i):
                x, y = chip_of(i)
                term = lax.dot_general(left(x, y, at.core), right[...], TN, preferred_element_type=jnp.float32)
                send(i).wait_recv()
                term = term + landing[x * 2 + y].astype(jnp.float32)
                mine(x * 2 + y)[...] = term.astype(jnp.bfloat16)

        def drain():
            @pl.loop(0, 8)
            def _(i):
                send(i).wait_send()

        return theirs, ours, drain

    def g_columns(x, y, core):
        return g_ref[x, :, pl.ds(pl.multiple_of(y * 512 + core * 256, 256), 256)]

    def normed_columns(x, y, core):
        return other[:, pl.ds(pl.multiple_of(x * 1024 + y * 512 + core * 256, 256), 256)]

    def in_other(x, y):
        return other.at[pl.ds(pl.multiple_of(y * 256, 256), 256), pl.ds(pl.multiple_of(x * 1024, 1024), 1024)]

    theirs_out, ours_out, drain_core = terms(0, as_arriving, g_columns, attended_ref, in_other, lambda j: out_mine.at[j], core_out)
    out_steps = scatter_wide(
        at, out_scatter, lambda dx, dy: out_mine.at[chip(dx, dy)], (ya_out, yb_out), via_out, x_out, gow_ref
    )
    load_normed = pltpu.make_async_copy(normed_hbm, other, local_sem.at[2])

    scale = HEAD_DIM**-0.5

    def gv_copies(pair):
        def copy(k, src, device):
            return pltpu.make_async_remote_copy(
                src_ref=src, dst_ref=src, send_sem=gv_send.at[k, pair], recv_sem=gv_recv.at[k, pair],
                device_id=at.narrow(device), device_id_type=MESH,
            )

        mine = gv_all.at[at.n, pair]
        on_p = gv_all.at[at.n_m, pair, pl.ds(0, part)]
        on_m = gv_all.at[at.n_p, pair, pl.ds(part, part)]
        return copy(0, mine, at.n_p), copy(1, mine, at.n_m), copy(2, on_p, at.n_p), copy(3, on_m, at.n_m)

    def forward_gv(pair):
        to_p, to_m, on_p, on_m = gv_copies(pair)
        to_p.wait_recv()
        on_p.start()
        to_m.wait_recv()
        on_m.start()

    def attend(pair):
        lanes = pl.ds(pair * 256, 256)
        total = jnp.zeros((tok, 256), jnp.float32)
        for b in range(4):
            block = weight[4 * b : 4 * b + 4, :, lanes].reshape(width, 256)
            total = total + jnp.dot(g_ref[b], block, preferred_element_type=jnp.float32)
        both = total.astype(jnp.bfloat16)
        for h in range(2):
            cols = pl.ds(pair * 256 + h * HEAD_DIM, HEAD_DIM)
            gout = both[:, h * HEAD_DIM : (h + 1) * HEAD_DIM]
            prob = probs[2 * pair + h]
            dprob = lax.dot_general(value_ref[:, cols], gout, NT, preferred_element_type=jnp.float32)
            wide_prob = prob.astype(jnp.float32)
            delta = jnp.sum(wide_prob * dprob, axis=0, keepdims=True)
            dscore = (wide_prob * (dprob - delta)).astype(jnp.bfloat16)
            gv = jnp.dot(prob, gout, preferred_element_type=jnp.float32).astype(jnp.bfloat16)
            gv_own[:, cols] = gv
            gv_all[at.n, pair, :, pl.ds(h * HEAD_DIM, HEAD_DIM)] = gv
            gk = jnp.dot(dscore, query_ref[:, cols], preferred_element_type=jnp.float32) * scale
            gk_ref[:, cols] = gk.astype(jnp.bfloat16)
            gq = lax.dot_general(dscore, key_ref[:, cols], TN, preferred_element_type=jnp.float32) * scale
            gq_ref[:, cols] = gq.astype(jnp.bfloat16)
        to_p, to_m, _, _ = gv_copies(pair)
        to_p.start()
        to_m.start()

    def load_tile(tile):
        return pltpu.make_async_copy(vw_all.at[pl.ds(4 * tile, 4)], core_out.at[pl.ds(4 * (tile % 2), 4)], tile_sem.at[tile % 2])

    theirs_value, ours_value, drain_value = terms(
        1, far_first, normed_columns, gv_own, lambda x, y: weight.at[x * 2 + y], lambda j: weight.at[8 + j], core_value
    )
    value_steps = scatter_wide(
        at, value_scatter, lambda dx, dy: weight.at[8 + chip(dx, dy)], (ya_val, yb_val), via_val, x_val, gvw_ref
    )
    def wait_gv():
        for pair in range(4):
            _, _, on_p, on_m = gv_copies(pair)
            on_p.wait_recv()
            on_m.wait_recv()

    def gin_copies(tile, y):
        def copy(k, src, dst, device):
            return pltpu.make_async_remote_copy(
                src_ref=src, dst_ref=dst, send_sem=gin_send.at[k, 2 * tile + y], recv_sem=gin_recv.at[k, 2 * tile + y],
                device_id=at.narrow(device), device_id_type=MESH,
            )

        def chunk(n, start, size):
            cols = pl.ds(pl.multiple_of(tile * 1024 + y * 512 + n * 128, 128), 128)
            return gin_hbm.at[pl.ds(start, size), cols]

        src, dst = hop.at[tile, :, pl.ds(y * 128, 128)], chunk(at.n, 0, tok)
        on_p, on_m = chunk(at.n_m, 0, part), chunk(at.n_p, part, part)
        own = pltpu.make_async_copy(src, dst, own_sem.at[2 * tile + y])
        return copy(0, src, dst, at.n_p), copy(1, src, dst, at.n_m), copy(2, on_p, on_p, at.n_p), copy(3, on_m, on_m, at.n_m), own

    def forward_gin(tile):
        for y in range(2):
            to_p, to_m, on_p, on_m, _ = gin_copies(tile, y)
            to_p.wait_recv()
            on_p.start()
            to_m.wait_recv()
            on_m.start()

    def gin(tile):
        load_tile(tile).wait()
        chunk = pl.multiple_of(at.n * 128, 128)
        low = g_ref[tile, :, pl.ds(chunk, 128)]
        high = g_ref[tile, :, pl.ds(pl.multiple_of(chunk + 512, 128), 128)]
        total = jnp.concatenate([low, high], axis=1).astype(jnp.float32)
        for z in range(4):
            for pair in range(4):
                block = core_out[
                    4 * (tile % 2) : 4 * (tile % 2) + 4, z * 64 : (z + 1) * 64, pair * 256 : (pair + 1) * 256
                ].reshape(256, 256)
                total = total + lax.dot_general(gv_all[z, pair], block, NT, preferred_element_type=jnp.float32)
        hop[tile] = total.astype(jnp.bfloat16)
        for y in range(2):
            to_p, to_m, _, _, own = gin_copies(tile, y)
            to_p.start()
            to_m.start()
            own.start()
        if tile < 2:
            load_tile(tile + 2).start()

    out_first, out_second_y, out_second_x, out_third, out_fourth, out_last = out_gather
    value_first, value_second_y, value_second_x, value_third, value_fourth, value_last = value_gather
    out_sum_a, out_sum_b, out_sum_second, out_sum_third, out_sum_fourth = out_steps
    value_sum_a, value_sum_b, value_sum_second, value_sum_third, value_sum_fourth = value_steps

    stores = [
        pltpu.make_async_copy(src, dst, store_sem.at[k])
        for k, (src, dst) in enumerate(((gq_ref, gq_hbm), (gk_ref, gk_hbm), (gow_ref, gow_hbm), (gvw_ref, gvw_hbm)))
    ]

    wait_loads()
    heads(0, 2)
    pack(0)
    wait_places()
    pack(1)
    unpack(0)
    out_second_y()
    out_second_x()
    pack(2)
    unpack(1)
    heads(2, 4)
    out_third()
    pack(3)
    wait_share()
    value_first()
    unpack(2)
    forward(0)
    unpack(3)
    out_fourth()
    forward(1)
    heads(4, 8)
    value_second_y()
    value_second_x()
    forward(2)
    drain_rows()
    theirs_out(0, 2)
    forward(3)
    theirs_out(2, 6)
    ours_out(0, 6)
    value_third()
    wait_gathered()
    out_last()
    attend(0)
    theirs_out(6, 8)
    ours_out(6, 8)
    out_sum_a()
    out_sum_b()
    drain_core()
    load_normed.start()
    attend(1)
    forward_gv(0)
    value_fourth()
    attend(2)
    forward_gv(1)
    out_sum_second()
    attend(3)
    stores[0].start()
    stores[1].start()
    forward_gv(2)
    out_sum_third()
    out_links.drain()
    load_normed.wait()
    theirs_value(0, 8)
    forward_gv(3)
    ours_value(0, 2)
    value_sum_a()
    ours_value(2, 8)
    value_sum_b()
    value_last()
    load_tile(0).start()
    load_tile(1).start()
    wait_gv()
    gin(0)
    gin(1)
    gin(2)
    gin(3)
    out_sum_fourth()
    stores[2].start()
    forward_gin(0)
    value_sum_second()
    forward_gin(1)
    forward_gin(2)
    value_sum_third()
    forward_gin(3)
    value_sum_fourth()
    stores[3].start()
    drain_value()
    for tile in range(4):
        for y in range(2):
            to_p, to_m, on_p, on_m, own = gin_copies(tile, y)
            on_p.wait_recv()
            on_m.wait_recv()
            own.wait()
            for copy in (to_p, to_m, on_p, on_m):
                copy.wait_send()
        for copy in gv_copies(tile):
            copy.wait_send()
    for h in range(2):
        for c in range(2):
            mine, remote, local = share(h, c)
            pl.when(jnp.logical_not(mine))(remote.wait_send)

    for used in (links, value_links, out_scatter, value_scatter):
        used.drain()
    for store in stores:
        store.wait()


def backward(tile, target, row, wo, vw, query, key, value, position, normed):
    tok, width = tile.shape
    rows = wo.shape[0]
    low, middle = split_rows(rows)
    chunks = 4
    bf16, f32, i32 = jnp.bfloat16, jnp.float32, jnp.int32
    dma = pltpu.SemaphoreType.DMA
    vmem = pl.BlockSpec(memory_space=pltpu.VMEM)
    hbm = pl.BlockSpec(memory_space=pl.ANY)

    def buffer(*shape):
        return pltpu.VMEM(shape, bf16)

    landing = [
        buffer(4, low, width),
        buffer(rows - low, width),
        buffer(3, 2, rows - middle, width),
        buffer(3, 2, rows - low, width),
    ]
    return pl.pallas_call(
        kernel,
        out_shape=(
            jax.ShapeDtypeStruct((tok, 4 * width), bf16),
            jax.ShapeDtypeStruct((tok, width), bf16),
            jax.ShapeDtypeStruct((tok, width), bf16),
            jax.ShapeDtypeStruct((rows, width), f32),
            jax.ShapeDtypeStruct((rows, width), f32),
            jax.ShapeDtypeStruct((16, rows, width), bf16),
        ),
        in_specs=[hbm, vmem, vmem, hbm, hbm, hbm, hbm, hbm, vmem, hbm],
        out_specs=(hbm,) * 6,
        scratch_shapes=[
            *[buffer(tok, width)] * 2,
            *[pltpu.VMEM((rows, width), f32)] * 2,
            buffer(4, tok, width),
            *[buffer(tok, width)] * 4,
            buffer(width // HEAD_DIM, tok, tok),
            buffer(16, rows, width),
            buffer(tok, 4 * width),
            *[buffer(8, rows, width)] * 3,
            *landing,
            *landing,
            buffer(tok, width),
            buffer(4, 4, tok, 256),
            buffer(chunks, tok, width // chunks),
            pltpu.VMEM((8, tok), i32),
            pltpu.VMEM((16, 8, 128), i32),
            pltpu.VMEM((8, tok), i32),
            pltpu.VMEM((16, 8, 128), i32),
            buffer(chunks, 16, PAD, width // chunks),
            pltpu.VMEM((16, 8, 128), i32),
            buffer(rows, width),
            *[dma((22,))] * 2,
            *[dma((20,))] * 4,
            *[dma((17,))] * 4,
            *[dma((chunks, 16))] * 2,
            *[dma((16,))] * 2,
            *[dma((4,))] * 2,
            *[dma((2, 8))] * 2,
            *[dma((4, 4))] * 2,
            *[dma((4, 8))] * 2,
            dma((8,)), dma((2,)), dma((3,)), dma((3,)), dma((4,)),
        ],
        compiler_params=pltpu.CompilerParams(
            collective_id=0, has_side_effects=True, vmem_limit_bytes=63 * 1024 * 1024
        ),
        name="relay_backward_and_sum",
    )(tile, target, row, wo, vw, query, key, value, position, normed)


def copy_kernel(count, *refs):
    sources, targets, held = refs[:count], refs[count : 2 * count], refs[2 * count : 3 * count]
    into_sem, out_sem = refs[3 * count :]
    steps = []
    for src, dst, buffer in zip(sources, targets, held):
        rows = src.shape[0] // (8 if src.shape[1] > 1024 else 2)
        for start in range(0, src.shape[0], rows):
            span, k = pl.ds(start, rows), len(steps)
            steps.append(
                (
                    pltpu.make_async_copy(src.at[span], buffer.at[span], into_sem.at[k]),
                    pltpu.make_async_copy(buffer.at[span], dst.at[span], out_sem.at[k]),
                )
            )
    for into, _ in steps:
        into.start()
    for into, out in steps:
        into.wait()
        out.start()
    for _, out in steps:
        out.wait()


def copied(arrays):
    hbm = pl.BlockSpec(memory_space=pl.ANY)
    return pl.pallas_call(
        functools.partial(copy_kernel, len(arrays)),
        out_shape=tuple(jax.ShapeDtypeStruct(array.shape, array.dtype) for array in arrays),
        in_specs=[hbm] * len(arrays),
        out_specs=(hbm,) * len(arrays),
        scratch_shapes=[pltpu.VMEM(array.shape, array.dtype) for array in arrays]
        + [pltpu.SemaphoreType.DMA((16,))] * 2,
        compiler_params=pltpu.CompilerParams(vmem_limit_bytes=60 * 1024 * 1024),
        name="copied",
    )(*arrays)


def shards(boundary_grad, tile_target, tile_row, normed_input, query, keys, values, positions, out_weight, value_weight):
    outputs = backward(
        boundary_grad[0], tile_target, tile_row, out_weight[0], value_weight[0], query[0], keys[0], values[0], positions,
        normed_input[0],
    )
    return tuple(output[None] for output in copied(outputs[:5]))


def solution(mesh):
    split = P("section", "wide", "narrow")
    rows = P("section", "wide")
    in_specs = (split, rows, rows, P("section", "wide", None), split, split, split, rows, split, split)
    out_specs = (P("section", "wide", None), split, split, split, split)
    return jax.shard_map(shards, mesh=mesh, in_specs=in_specs, out_specs=out_specs, check_vma=False)
```

```python
import functools

import jax
import jax.numpy as jnp
from jax import lax
from jax.experimental import pallas as pl
from jax.experimental.pallas import tpu as pltpu
from jax.sharding import PartitionSpec as P

HEAD_DIM = 128
MESH = pl.DeviceIdType.MESH
NT = (((1,), (1,)), ((), ()))
TN = (((0,), (0,)), ((), ()))
SLOTS = 48
PAD = 64


class Place:
    def __init__(self):
        self.s = lax.axis_index("section")
        self.w = lax.axis_index("wide")
        self.n = lax.axis_index("narrow")
        self.core = self.w % 2
        self.y = (self.w // 2) % 2
        self.x = self.w // 4
        self.w_xp = (self.w + 4) % 16
        self.w_xm = (self.w + 12) % 16
        self.w_x2 = (self.w + 8) % 16
        self.w_y = self.w + 2 - 4 * self.y
        self.w_core = self.w + 1 - 2 * self.core
        self.y_xp = (self.w_y + 4) % 16
        self.y_xm = (self.w_y + 12) % 16
        self.y_x2 = (self.w_y + 8) % 16
        self.n_p = (self.n + 1) % 4
        self.n_m = (self.n + 3) % 4
        self.n_2 = (self.n + 2) % 4

    def wide(self, w):
        return (self.s, w, self.n)

    def narrow(self, n):
        return (self.s, self.w, n)


class Links:
    def __init__(self, send_sem, recv_sem):
        self.send_sem, self.recv_sem, self.count, self.sent = send_sem, recv_sem, 0, []

    def put(self, src, dst, device):
        copy = pltpu.make_async_remote_copy(
            src_ref=src,
            dst_ref=dst,
            send_sem=self.send_sem.at[self.count],
            recv_sem=self.recv_sem.at[self.count],
            device_id=device,
            device_id_type=MESH,
        )
        copy.start()
        self.count += 1
        self.sent.append(copy)
        return copy

    def drain(self):
        for copy in self.sent:
            copy.wait_send()


def greet(devices):
    barrier = pltpu.get_barrier_semaphore()
    for device in devices:
        pl.semaphore_signal(barrier, inc=1, device_id=device, device_id_type=MESH)
    return barrier


def split_rows(rows):
    low = rows * 7 // 16
    return low, low + rows // 4


def gather_wide(at, links, own, full, local_sem):
    rows = own.shape[0]
    low, middle = split_rows(rows)
    lower, upper = pl.ds(0, low), pl.ds(low, rows - low)
    third, fourth = pl.ds(low, middle - low), pl.ds(middle, rows - middle)
    one, two = pl.ds(0, rows // 2), pl.ds(rows // 2, rows // 2)
    xp, xm, yy, cc = (at.wide(w) for w in (at.w_xp, at.w_xm, at.w_y, at.w_core))

    def send(w, device, rows=None):
        ref = full.at[w] if rows is None else full.at[w, rows]
        return links.put(ref, ref, device)

    state = {}

    def first():
        state["own"] = pltpu.make_async_copy(own, full.at[at.w], local_sem)
        state["own"].start()
        state["y"] = links.put(own, full.at[at.w], yy)
        state["xp"] = links.put(own, full.at[at.w], xp)
        state["xm"] = links.put(own, full.at[at.w], xm)
        state["core"] = links.put(own, full.at[at.w], cc)

    def second_y():
        state["y"].wait_recv()
        state["b_p"] = send(at.w_y, xp, upper)
        state["b_m"] = send(at.w_y, xm, upper)
        state["c_y"] = send(at.w_y, cc)

    def second_x():
        state["xp"].wait_recv()
        state["f_p"] = send(at.w_xm, xp, one)
        state["g_m"] = send(at.w_xm, yy, lower)
        state["c_m"] = send(at.w_xm, cc)
        state["xm"].wait_recv()
        state["f_m"] = send(at.w_xp, xm, two)
        state["g_p"] = send(at.w_xp, yy, lower)
        state["c_p"] = send(at.w_xp, cc)

    def third_step():
        state["b_p"].wait_recv()
        state["h_p"] = send(at.y_xm, xp, third)
        state["b_m"].wait_recv()
        state["h_m"] = send(at.y_xp, xm, fourth)
        state["f_p"].wait_recv()
        state["g_2"] = send(at.w_x2, yy, lower)
        state["f_m"].wait_recv()
        state["c_2"] = send(at.w_x2, cc)

    def fourth_step():
        state["g_m"].wait_recv()
        state["e_m"] = send(at.y_xm, cc)
        state["g_p"].wait_recv()
        state["e_p"] = send(at.y_xp, cc)
        state["h_p"].wait_recv()
        state["h_m"].wait_recv()
        state["g_2"].wait_recv()
        state["e_2"] = send(at.y_x2, cc)

    def last():
        state["own"].wait()
        for name in ("core", "c_y", "c_m", "c_p", "c_2", "e_m", "e_p", "e_2"):
            state[name].wait_recv()

    return first, second_y, second_x, third_step, fourth_step, last


def attention_forward(head, query_ref, key_ref, value_ref, allowed, probs_ref, attended_ref):
    lanes = pl.ds(pl.multiple_of(head * HEAD_DIM, HEAD_DIM), HEAD_DIM)
    scores = lax.dot_general(key_ref[:, lanes], query_ref[:, lanes], NT, preferred_element_type=jnp.float32)
    scores = jnp.where(allowed, scores * HEAD_DIM**-0.5, -1e30)
    weights = jnp.exp(scores - jnp.max(scores, axis=0, keepdims=True))
    probs = (weights / jnp.sum(weights, axis=0, keepdims=True)).astype(jnp.bfloat16)
    probs_ref[head] = probs
    attended = lax.dot_general(probs, value_ref[:, lanes], TN, preferred_element_type=jnp.float32)
    attended_ref[:, lanes] = attended.astype(jnp.bfloat16)


def scatter_wide(at, links, mine, from_y, via, from_x, result):
    rows = result.shape[0]
    low, middle = split_rows(rows)
    lower, upper = pl.ds(0, low), pl.ds(low, rows - low)
    low_parts = pl.ds(0, rows // 4), pl.ds(rows // 4, low - rows // 4)
    high_parts = pl.ds(low, middle - low), pl.ds(middle, rows - middle)
    xp, xm, yy = (at.wide(w) for w in (at.w_xp, at.w_xm, at.w_y))
    ya, yb = from_y
    state = {}

    def add(dx, dy, rows, *others):
        ref = mine(dx, dy).at[rows]
        total = ref[...].astype(jnp.float32)
        for other in others:
            total = total + other[...].astype(jnp.float32)
        return ref, total

    def add_into(dx, dy, rows, *others):
        ref, total = add(dx, dy, rows, *others)
        ref[...] = total.astype(jnp.bfloat16)

    def across(name, slot, dx_dy, parts):
        for k, device in ((0, xp), (1, xm)):
            landing = via.at[slot, k, pl.ds(0, parts[k].size)]
            state[name, k] = links.put(mine(*dx_dy).at[parts[k]], landing, device)

    def first_a():
        state["ya2"] = links.put(mine(2, 1).at[lower], ya.at[2], yy)
        across("vb1", 1, (2, 1), high_parts)
        across("vb0", 0, (2, 0), high_parts)

    def first_b():
        for dx in (1, 3, 0):
            state["ya%d" % dx] = links.put(mine(dx, 1).at[lower], ya.at[dx], yy)

    def onward(name, slot, dy, parts, rows):
        for k, dx, device in ((0, 1, xp), (1, 3, xm)):
            state[name, k].wait_recv()
            add_into(dx, dy, parts[k], via.at[slot, k, pl.ds(0, parts[k].size)])
            landing = from_x.at[slot, k, pl.ds(0, rows.size)]
            state["r" + name, k] = links.put(mine(dx, dy).at[rows], landing, device)

    def second():
        state["ya2"].wait_recv()
        add_into(2, 0, lower, ya.at[2])
        across("va", 2, (2, 0), low_parts)
        onward("vb1", 1, 1, high_parts, upper)
        onward("vb0", 0, 0, high_parts, upper)

    def upper_from_x(slot):
        return [from_x.at[slot, k] for k in range(2)]

    def third():
        for dx in (1, 3):
            state["ya%d" % dx].wait_recv()
            add_into(dx, 0, lower, ya.at[dx])
        onward("va", 2, 0, low_parts, lower)
        for k in range(2):
            state["rvb1", k].wait_recv()
        add_into(0, 1, upper, *upper_from_x(1))
        state["yb"] = links.put(mine(0, 1).at[upper], yb, yy)

    def fourth():
        state["ya0"].wait_recv()
        for k in range(2):
            state["rva", k].wait_recv()
        lower_from_x = [from_x.at[2, k, pl.ds(0, low)] for k in range(2)]
        result[lower, :] = add(0, 0, lower, ya.at[0], *lower_from_x)[1]
        for k in range(2):
            state["rvb0", k].wait_recv()
        state["yb"].wait_recv()
        result[upper, :] = add(0, 0, upper, yb, *upper_from_x(0))[1]

    return first_a, first_b, second, third, fourth


def kernel(
    tile_hbm, target_ref, row_ref, wo_hbm, vw_hbm, query_hbm, key_hbm, value_hbm, position_ref, normed_hbm,
    gin_hbm, gq_hbm, gk_hbm, gow_hbm, gvw_hbm, vw_all,
    gq_ref, gk_ref, gow_ref, gvw_ref,
    g_ref, query_ref, key_ref, value_ref, attended_ref, probs, weight, other, out_mine, core_out, core_value,
    ya_out, yb_out, via_out, x_out, ya_val, yb_val, via_val, x_val, gv_own, gv_all,
    hop, hop_slot, hop_places, slots, places, landed, landed_places, vw_own,
    relay_send, relay_recv, out_send, out_recv, value_send, value_recv, out_sum_send, out_sum_recv,
    value_sum_send, value_sum_recv, data_send, data_recv, place_send, place_recv, share_send, share_recv,
    core_send, core_recv, gv_send, gv_recv, gin_send, gin_recv, own_sem, tile_sem, local_sem, load_sem, store_sem,
):
    at = Place()
    loads = [
        pltpu.make_async_copy(src, dst, load_sem.at[k])
        for k, (src, dst) in enumerate(((query_hbm, query_ref), (key_hbm, key_ref), (value_hbm, value_ref)))
    ]
    for load in loads:
        load.start()
    groups = 16
    tok, width = tile_hbm.shape
    chunks, _, cols = hop.shape
    across = (1 - at.s, at.w_y, at.n)
    barrier = greet(
        [across]
        + [at.wide((at.w + i) % groups) for i in range(1, groups)]
        + [(at.s, w, n) for w in (at.w, at.w_core) for n in (at.n_p, at.n_m, at.n_2)]
    )
    target = target_ref[...]
    group = lax.broadcasted_iota(jnp.int32, (groups, tok), 0)
    member = jnp.where(group == target, 1.0, 0.0).astype(jnp.float32)
    before = jnp.where(
        lax.broadcasted_iota(jnp.int32, (tok, tok), 0) < lax.broadcasted_iota(jnp.int32, (tok, tok), 1), 1.0, 0.0
    ).astype(jnp.bfloat16)
    earlier = jnp.dot(member.astype(jnp.bfloat16), before, preferred_element_type=jnp.float32)
    within = jnp.sum(earlier * member, axis=0, keepdims=True).astype(jnp.int32)
    slots[...] = jnp.broadcast_to(target * PAD + within, slots.shape)
    lane = within + PAD * (at.w % 2)
    to_lane = jnp.where(
        lax.broadcasted_iota(jnp.int32, (128, tok), 0) == lane, 1.0, 0.0
    ).astype(jnp.bfloat16)
    place = row_ref[...] + 1
    high = (place // 32).astype(jnp.float32)
    low = (place % 32).astype(jnp.float32)
    high = lax.dot_general((member * high).astype(jnp.bfloat16), to_lane, NT, preferred_element_type=jnp.float32)
    low = lax.dot_general((member * low).astype(jnp.bfloat16), to_lane, NT, preferred_element_type=jnp.float32)
    lanes = (high * 32.0 + low).astype(jnp.int32)
    places[...] = jnp.broadcast_to(lanes[:, None, :], places.shape)
    landed[:, :, SLOTS:, :] = jnp.zeros((chunks, groups, PAD - SLOTS, cols), landed.dtype)
    pl.semaphore_wait(barrier, 1 + 15 + 6)

    links = Links(relay_send, relay_recv)
    out_links = Links(out_send, out_recv)
    value_links = Links(value_send, value_recv)
    hop_index = [links.put(slots, hop_slot, across), links.put(places, hop_places, across)]
    hop_data = [links.put(tile_hbm.at[:, pl.ds(k * cols, cols)], hop.at[k], across) for k in range(chunks)]

    half_chunk = vw_hbm.shape[0] // 4

    def share(h, c):
        w, n = at.w - at.core + c, 2 * at.core + h
        src = vw_hbm.at[pl.ds((2 * h + c) * half_chunk, half_chunk)]
        dst = vw_own.at[pl.ds(pl.multiple_of(at.n * half_chunk, half_chunk), half_chunk)]
        mine = (at.core == c) & (at.n == n)
        remote = pltpu.make_async_remote_copy(
            src_ref=src, dst_ref=dst, send_sem=share_send.at[2 * h + c], recv_sem=share_recv.at[at.n],
            device_id=(at.s, w, n), device_id_type=MESH,
        )
        return mine, remote, lambda: pltpu.make_async_copy(src, dst, share_recv.at[at.n]).start()

    out_gather = gather_wide(at, out_links, wo_hbm, weight, local_sem.at[0])
    value_gather = gather_wide(at, value_links, vw_own, vw_all, local_sem.at[1])
    out_gather[0]()
    for h in range(2):
        for c in range(2):
            mine, remote, local = share(h, c)
            pl.when(mine)(local)
            pl.when(jnp.logical_not(mine))(remote.start)

    hop_index[0].wait_recv()
    slot = hop_slot[0:1, :]

    def choose(r):
        return out_mine.at[4 + r // 2, :, pl.ds((r % 2) * tok, tok)]

    for r in range(4):
        wanted = lax.broadcasted_iota(jnp.int32, (256, tok), 0) + r * 256
        choose(r)[...] = jnp.where(wanted == slot, 1.0, 0.0).astype(jnp.bfloat16)

    hop_index[1].wait_recv()

    def send_place(i):
        t = (at.w + i) % groups
        return pltpu.make_async_remote_copy(
            src_ref=hop_places.at[t], dst_ref=landed_places.at[at.w],
            send_sem=place_send.at[t], recv_sem=place_recv.at[at.w],
            device_id=at.wide(t), device_id_type=MESH,
        )

    def from_packed(k, t):
        rows = pl.ds(pl.multiple_of((t % 4) * PAD, PAD), SLOTS)
        return out_mine.at[t // 4, rows, pl.ds(k * cols, cols)], landed.at[k, at.w, pl.ds(0, SLOTS)]

    def send_rows(k, i):
        t = (at.w + i) % groups
        src, dst = from_packed(k, t)
        return pltpu.make_async_remote_copy(
            src_ref=src, dst_ref=dst, send_sem=data_send.at[k, t], recv_sem=data_recv.at[k, at.w],
            device_id=at.wide(t), device_id_type=MESH,
        )

    pltpu.make_async_copy(hop_places.at[at.w], landed_places.at[at.w], place_recv.at[at.w]).start()

    @pl.loop(1, groups)
    def _(i):
        send_place(i).start()

    def pack(k):
        hop_data[k].wait_recv()
        for r in range(4):
            rows = jnp.dot(choose(r)[...], hop[k], preferred_element_type=jnp.float32)
            out_mine[r, :, pl.ds(k * cols, cols)] = rows.astype(jnp.bfloat16)
        src, dst = from_packed(k, at.w)
        pltpu.make_async_copy(src, dst, data_recv.at[k, at.w]).start()

        @pl.loop(1, groups)
        def _(i):
            send_rows(k, i).start()

    part = tok // 2
    z_p, z_m, on_p, on_m = [], [], [], []

    def unpack(k):
        @pl.loop(0, groups)
        def _(i):
            piece = landed.at[k, i, pl.ds(0, SLOTS)]
            pltpu.make_async_copy(piece, piece, data_recv.at[k, i]).wait()

        rows = landed[k].reshape(groups * PAD, cols)
        for r in range(2):
            placed = jnp.dot(out_mine[6 + r], rows, preferred_element_type=jnp.float32)
            g_ref[at.n, pl.ds(r * part, part), pl.ds(k * cols, cols)] = placed.astype(jnp.bfloat16)
        ref = g_ref.at[at.n, :, pl.ds(k * cols, cols)]
        z_p.append(links.put(ref, ref, at.narrow(at.n_p)))
        z_m.append(links.put(ref, ref, at.narrow(at.n_m)))

    def forward(k):
        z_p[k].wait_recv()
        ref = g_ref.at[at.n_m, pl.ds(0, part), pl.ds(k * cols, cols)]
        on_p.append(links.put(ref, ref, at.narrow(at.n_p)))
        z_m[k].wait_recv()
        ref = g_ref.at[at.n_p, pl.ds(part, part), pl.ds(k * cols, cols)]
        on_m.append(links.put(ref, ref, at.narrow(at.n_m)))

    key_at = lax.broadcasted_iota(jnp.int32, (tok, tok), 0)
    query_at = lax.broadcasted_iota(jnp.int32, (tok, tok), 1)
    earliest = lax.broadcasted_iota(jnp.int32, (1, tok), 1) - position_ref[...]

    def heads(first, last):
        @pl.loop(first, last)
        def _(head):
            allowed = (key_at <= query_at) & (key_at >= earliest)
            attention_forward(head, query_ref, key_ref, value_ref, allowed, probs, attended_ref)

    def wait_places():
        @pl.loop(0, groups)
        def _(i):
            piece = landed_places.at[i]
            pltpu.make_async_copy(piece, piece, place_recv.at[i]).wait()

        arrived = landed_places[...].reshape(groups // 2, 2, 8, 128)
        arrived = (arrived[:, 0] + arrived[:, 1])[:, 0, :]
        for r in range(2):
            token = lax.broadcasted_iota(jnp.int32, (part, 128), 0) + (1 + r * part)
            for k in range(groups // 2):
                here = jnp.where(token == arrived[k : k + 1, :], 1.0, 0.0)
                out_mine[6 + r, :, pl.ds(k * 128, 128)] = here.astype(jnp.bfloat16)

    def wait_loads():
        for load in loads:
            load.wait()

    def wait_share():
        for b in range(4):
            piece = vw_own.at[pl.ds(b * half_chunk, half_chunk)]
            pltpu.make_async_copy(piece, piece, share_recv.at[b]).wait()

    def drain_rows():
        @pl.loop(1, groups)
        def _(i):
            send_place(i).wait_send()
            for k in range(chunks):
                send_rows(k, i).wait_send()

    def wait_gathered():
        for k in range(chunks):
            on_p[k].wait_recv()
            on_m[k].wait_recv()

    out_scatter = Links(out_sum_send, out_sum_recv)
    value_scatter = Links(value_sum_send, value_sum_recv)

    def chip(dx, dy):
        y = at.y if dy == 0 else 1 - at.y
        return ((at.x + dx) % 4) * 2 + y

    def far_first(i):
        return (at.x + 2 + i // 2) % 4, (at.y + 1 + i) % 2

    def as_arriving(i):
        k = i // 2
        return (at.n + k + k // 2 - 2 * (k // 3)) % 4, i % 2

    def terms(which, chip_of, left, right, to_core, mine, landing):
        def send(i):
            x, y = chip_of(i)
            return pltpu.make_async_remote_copy(
                src_ref=to_core(x, y), dst_ref=landing.at[x * 2 + y],
                send_sem=core_send.at[which, i], recv_sem=core_recv.at[which, i],
                device_id=at.wide(at.w_core), device_id_type=MESH,
            )

        def theirs(first, last):
            @pl.loop(first, last)
            def _(i):
                x, y = chip_of(i)
                term = lax.dot_general(left(x, y, 1 - at.core), right[...], TN, preferred_element_type=jnp.float32)
                to_core(x, y)[...] = term.astype(jnp.bfloat16)
                send(i).start()

        def ours(first, last):
            @pl.loop(first, last)
            def _(i):
                x, y = chip_of(i)
                term = lax.dot_general(left(x, y, at.core), right[...], TN, preferred_element_type=jnp.float32)
                send(i).wait_recv()
                term = term + landing[x * 2 + y].astype(jnp.float32)
                mine(x * 2 + y)[...] = term.astype(jnp.bfloat16)

        def drain():
            @pl.loop(0, 8)
            def _(i):
                send(i).wait_send()

        return theirs, ours, drain

    def g_columns(x, y, core):
        return g_ref[x, :, pl.ds(pl.multiple_of(y * 512 + core * 256, 256), 256)]

    def normed_columns(x, y, core):
        return other[:, pl.ds(pl.multiple_of(x * 1024 + y * 512 + core * 256, 256), 256)]

    def in_other(x, y):
        return other.at[pl.ds(pl.multiple_of(y * 256, 256), 256), pl.ds(pl.multiple_of(x * 1024, 1024), 1024)]

    theirs_out, ours_out, drain_core = terms(0, as_arriving, g_columns, attended_ref, in_other, lambda j: out_mine.at[j], core_out)
    out_steps = scatter_wide(
        at, out_scatter, lambda dx, dy: out_mine.at[chip(dx, dy)], (ya_out, yb_out), via_out, x_out, gow_ref
    )
    load_normed = pltpu.make_async_copy(normed_hbm, other, local_sem.at[2])

    scale = HEAD_DIM**-0.5

    def gv_copies(pair):
        def copy(k, src, device):
            return pltpu.make_async_remote_copy(
                src_ref=src, dst_ref=src, send_sem=gv_send.at[k, pair], recv_sem=gv_recv.at[k, pair],
                device_id=at.narrow(device), device_id_type=MESH,
            )

        mine = gv_all.at[at.n, pair]
        on_p = gv_all.at[at.n_m, pair, pl.ds(0, part)]
        on_m = gv_all.at[at.n_p, pair, pl.ds(part, part)]
        return copy(0, mine, at.n_p), copy(1, mine, at.n_m), copy(2, on_p, at.n_p), copy(3, on_m, at.n_m)

    def forward_gv(pair):
        to_p, to_m, on_p, on_m = gv_copies(pair)
        to_p.wait_recv()
        on_p.start()
        to_m.wait_recv()
        on_m.start()

    def gv_pair(pair):
        lanes = pl.ds(pair * 256, 256)
        total = jnp.zeros((tok, 256), jnp.float32)
        for b in range(4):
            block = weight[4 * b : 4 * b + 4, :, lanes].reshape(width, 256)
            total = total + jnp.dot(g_ref[b], block, preferred_element_type=jnp.float32)
        both = total.astype(jnp.bfloat16)
        gq_ref[:, lanes] = both
        for h in range(2):
            gout = both[:, h * HEAD_DIM : (h + 1) * HEAD_DIM]
            gv = jnp.dot(probs[2 * pair + h], gout, preferred_element_type=jnp.float32).astype(jnp.bfloat16)
            gv_own[:, pl.ds(pair * 256 + h * HEAD_DIM, HEAD_DIM)] = gv
            gv_all[at.n, pair, :, pl.ds(h * HEAD_DIM, HEAD_DIM)] = gv
        to_p, to_m, _, _ = gv_copies(pair)
        to_p.start()
        to_m.start()

    def score(pair):
        for h in range(2):
            cols = pl.ds(pair * 256 + h * HEAD_DIM, HEAD_DIM)
            prob = probs[2 * pair + h]
            dprob = lax.dot_general(value_ref[:, cols], gq_ref[:, cols], NT, preferred_element_type=jnp.float32)
            wide_prob = prob.astype(jnp.float32)
            delta = jnp.sum(wide_prob * dprob, axis=0, keepdims=True)
            dscore = (wide_prob * (dprob - delta)).astype(jnp.bfloat16)
            gk = jnp.dot(dscore, query_ref[:, cols], preferred_element_type=jnp.float32) * scale
            gk_ref[:, cols] = gk.astype(jnp.bfloat16)
            gq = lax.dot_general(dscore, key_ref[:, cols], TN, preferred_element_type=jnp.float32) * scale
            gq_ref[:, cols] = gq.astype(jnp.bfloat16)

    def load_tile(tile):
        return pltpu.make_async_copy(vw_all.at[pl.ds(4 * tile, 4)], core_out.at[pl.ds(4 * (tile % 2), 4)], tile_sem.at[tile % 2])

    theirs_value, ours_value, drain_value = terms(
        1, far_first, normed_columns, gv_own, lambda x, y: weight.at[x * 2 + y], lambda j: weight.at[8 + j], core_value
    )
    value_steps = scatter_wide(
        at, value_scatter, lambda dx, dy: weight.at[8 + chip(dx, dy)], (ya_val, yb_val), via_val, x_val, gvw_ref
    )
    def wait_gv():
        for pair in range(4):
            _, _, on_p, on_m = gv_copies(pair)
            on_p.wait_recv()
            on_m.wait_recv()

    def gin_copies(tile, y):
        def copy(k, src, dst, device):
            return pltpu.make_async_remote_copy(
                src_ref=src, dst_ref=dst, send_sem=gin_send.at[k, 2 * tile + y], recv_sem=gin_recv.at[k, 2 * tile + y],
                device_id=at.narrow(device), device_id_type=MESH,
            )

        def chunk(n, start, size):
            cols = pl.ds(pl.multiple_of(tile * 1024 + y * 512 + n * 128, 128), 128)
            return gin_hbm.at[pl.ds(start, size), cols]

        src, dst = hop.at[tile, :, pl.ds(y * 128, 128)], chunk(at.n, 0, tok)
        on_p, on_m = chunk(at.n_m, 0, part), chunk(at.n_p, part, part)
        own = pltpu.make_async_copy(src, dst, own_sem.at[2 * tile + y])
        return copy(0, src, dst, at.n_p), copy(1, src, dst, at.n_m), copy(2, on_p, on_p, at.n_p), copy(3, on_m, on_m, at.n_m), own

    def forward_gin(tile):
        for y in range(2):
            to_p, to_m, on_p, on_m, _ = gin_copies(tile, y)
            to_p.wait_recv()
            on_p.start()
            to_m.wait_recv()
            on_m.start()

    def gin(tile):
        load_tile(tile).wait()
        chunk = pl.multiple_of(at.n * 128, 128)
        low = g_ref[tile, :, pl.ds(chunk, 128)]
        high = g_ref[tile, :, pl.ds(pl.multiple_of(chunk + 512, 128), 128)]
        total = jnp.concatenate([low, high], axis=1).astype(jnp.float32)
        for z in range(4):
            for pair in range(4):
                block = core_out[
                    4 * (tile % 2) : 4 * (tile % 2) + 4, z * 64 : (z + 1) * 64, pair * 256 : (pair + 1) * 256
                ].reshape(256, 256)
                total = total + lax.dot_general(gv_all[z, pair], block, NT, preferred_element_type=jnp.float32)
        hop[tile] = total.astype(jnp.bfloat16)
        for y in range(2):
            to_p, to_m, _, _, own = gin_copies(tile, y)
            to_p.start()
            to_m.start()
            own.start()
        if tile < 2:
            load_tile(tile + 2).start()

    out_first, out_second_y, out_second_x, out_third, out_fourth, out_last = out_gather
    value_first, value_second_y, value_second_x, value_third, value_fourth, value_last = value_gather
    out_sum_a, out_sum_b, out_sum_second, out_sum_third, out_sum_fourth = out_steps
    value_sum_a, value_sum_b, value_sum_second, value_sum_third, value_sum_fourth = value_steps

    stores = [
        pltpu.make_async_copy(src, dst, store_sem.at[k])
        for k, (src, dst) in enumerate(((gq_ref, gq_hbm), (gk_ref, gk_hbm), (gow_ref, gow_hbm), (gvw_ref, gvw_hbm)))
    ]

    wait_loads()
    heads(0, 2)
    pack(0)
    wait_places()
    pack(1)
    unpack(0)
    out_second_y()
    out_second_x()
    pack(2)
    unpack(1)
    heads(2, 4)
    out_third()
    pack(3)
    wait_share()
    value_first()
    unpack(2)
    forward(0)
    unpack(3)
    out_fourth()
    forward(1)
    heads(4, 8)
    value_second_y()
    value_second_x()
    forward(2)
    drain_rows()
    theirs_out(0, 2)
    forward(3)
    theirs_out(2, 6)
    ours_out(0, 6)
    wait_gathered()
    out_last()
    gv_pair(0)
    score(0)
    value_third()
    theirs_out(6, 8)
    ours_out(6, 8)
    out_sum_a()
    out_sum_b()
    drain_core()
    load_normed.start()
    gv_pair(1)
    score(1)
    forward_gv(0)
    value_fourth()
    gv_pair(2)
    score(2)
    forward_gv(1)
    out_sum_second()
    gv_pair(3)
    score(3)
    stores[0].start()
    stores[1].start()
    forward_gv(2)
    out_sum_third()
    out_links.drain()
    load_normed.wait()
    theirs_value(0, 8)
    forward_gv(3)
    ours_value(0, 2)
    value_sum_a()
    ours_value(2, 8)
    value_sum_b()
    value_last()
    load_tile(0).start()
    load_tile(1).start()
    wait_gv()
    gin(0)
    gin(1)
    gin(2)
    gin(3)
    out_sum_fourth()
    stores[2].start()
    forward_gin(0)
    value_sum_second()
    forward_gin(1)
    forward_gin(2)
    value_sum_third()
    forward_gin(3)
    value_sum_fourth()
    stores[3].start()
    drain_value()
    for tile in range(4):
        for y in range(2):
            to_p, to_m, on_p, on_m, own = gin_copies(tile, y)
            on_p.wait_recv()
            on_m.wait_recv()
            own.wait()
            for copy in (to_p, to_m, on_p, on_m):
                copy.wait_send()
        for copy in gv_copies(tile):
            copy.wait_send()
    for h in range(2):
        for c in range(2):
            mine, remote, local = share(h, c)
            pl.when(jnp.logical_not(mine))(remote.wait_send)

    for used in (links, value_links, out_scatter, value_scatter):
        used.drain()
    for store in stores:
        store.wait()


def backward(tile, target, row, wo, vw, query, key, value, position, normed):
    tok, width = tile.shape
    rows = wo.shape[0]
    low, middle = split_rows(rows)
    chunks = 4
    bf16, f32, i32 = jnp.bfloat16, jnp.float32, jnp.int32
    dma = pltpu.SemaphoreType.DMA
    vmem = pl.BlockSpec(memory_space=pltpu.VMEM)
    hbm = pl.BlockSpec(memory_space=pl.ANY)

    def buffer(*shape):
        return pltpu.VMEM(shape, bf16)

    landing = [
        buffer(4, low, width),
        buffer(rows - low, width),
        buffer(3, 2, rows - middle, width),
        buffer(3, 2, rows - low, width),
    ]
    return pl.pallas_call(
        kernel,
        out_shape=(
            jax.ShapeDtypeStruct((tok, 4 * width), bf16),
            jax.ShapeDtypeStruct((tok, width), bf16),
            jax.ShapeDtypeStruct((tok, width), bf16),
            jax.ShapeDtypeStruct((rows, width), f32),
            jax.ShapeDtypeStruct((rows, width), f32),
            jax.ShapeDtypeStruct((16, rows, width), bf16),
        ),
        in_specs=[hbm, vmem, vmem, hbm, hbm, hbm, hbm, hbm, vmem, hbm],
        out_specs=(hbm,) * 6,
        scratch_shapes=[
            *[buffer(tok, width)] * 2,
            *[pltpu.VMEM((rows, width), f32)] * 2,
            buffer(4, tok, width),
            *[buffer(tok, width)] * 4,
            buffer(width // HEAD_DIM, tok, tok),
            buffer(16, rows, width),
            buffer(tok, 4 * width),
            *[buffer(8, rows, width)] * 3,
            *landing,
            *landing,
            buffer(tok, width),
            buffer(4, 4, tok, 256),
            buffer(chunks, tok, width // chunks),
            pltpu.VMEM((8, tok), i32),
            pltpu.VMEM((16, 8, 128), i32),
            pltpu.VMEM((8, tok), i32),
            pltpu.VMEM((16, 8, 128), i32),
            buffer(chunks, 16, PAD, width // chunks),
            pltpu.VMEM((16, 8, 128), i32),
            buffer(rows, width),
            *[dma((22,))] * 2,
            *[dma((20,))] * 4,
            *[dma((17,))] * 4,
            *[dma((chunks, 16))] * 2,
            *[dma((16,))] * 2,
            *[dma((4,))] * 2,
            *[dma((2, 8))] * 2,
            *[dma((4, 4))] * 2,
            *[dma((4, 8))] * 2,
            dma((8,)), dma((2,)), dma((3,)), dma((3,)), dma((4,)),
        ],
        compiler_params=pltpu.CompilerParams(
            collective_id=0, has_side_effects=True, vmem_limit_bytes=63 * 1024 * 1024
        ),
        name="relay_backward_and_sum",
    )(tile, target, row, wo, vw, query, key, value, position, normed)


def copy_kernel(count, *refs):
    sources, targets, held = refs[:count], refs[count : 2 * count], refs[2 * count : 3 * count]
    into_sem, out_sem = refs[3 * count :]
    steps = []
    for src, dst, buffer in zip(sources, targets, held):
        rows = src.shape[0] // (8 if src.shape[1] > 1024 else 2)
        for start in range(0, src.shape[0], rows):
            span, k = pl.ds(start, rows), len(steps)
            steps.append(
                (
                    pltpu.make_async_copy(src.at[span], buffer.at[span], into_sem.at[k]),
                    pltpu.make_async_copy(buffer.at[span], dst.at[span], out_sem.at[k]),
                )
            )
    for into, _ in steps:
        into.start()
    for into, out in steps:
        into.wait()
        out.start()
    for _, out in steps:
        out.wait()


def copied(arrays):
    hbm = pl.BlockSpec(memory_space=pl.ANY)
    return pl.pallas_call(
        functools.partial(copy_kernel, len(arrays)),
        out_shape=tuple(jax.ShapeDtypeStruct(array.shape, array.dtype) for array in arrays),
        in_specs=[hbm] * len(arrays),
        out_specs=(hbm,) * len(arrays),
        scratch_shapes=[pltpu.VMEM(array.shape, array.dtype) for array in arrays]
        + [pltpu.SemaphoreType.DMA((16,))] * 2,
        compiler_params=pltpu.CompilerParams(vmem_limit_bytes=60 * 1024 * 1024),
        name="copied",
    )(*arrays)


def shards(boundary_grad, tile_target, tile_row, normed_input, query, keys, values, positions, out_weight, value_weight):
    outputs = backward(
        boundary_grad[0], tile_target, tile_row, out_weight[0], value_weight[0], query[0], keys[0], values[0], positions,
        normed_input[0],
    )
    return tuple(output[None] for output in copied(outputs[:5]))


def solution(mesh):
    split = P("section", "wide", "narrow")
    rows = P("section", "wide")
    in_specs = (split, rows, rows, P("section", "wide", None), split, split, split, rows, split, split)
    out_specs = (P("section", "wide", None), split, split, split, split)
    return jax.shard_map(shards, mesh=mesh, in_specs=in_specs, out_specs=out_specs, check_vma=False)
```
